128 devices in a mesh: seq: 64 (over x, z, y), head: 2 (over core).
Axes of the slice: x: 4, y: 4, z: 4, core: 2. Of those that a mesh axis runs over, the one named last changes fastest.
Arguments:
- layer_input: bfloat16 [2, 8192, 2048], P(None, 'seq', 'head'), may hold values from -6 to 6
- w_q: bfloat16 [2048, 2048], P('seq', 'head'), may hold values from -0.125 to 0.125
- w_f: bfloat16 [2048, 2048], P('seq', 'head'), may hold values from -0.125 to 0.125
- w_i: bfloat16 [2048, 2048], P('seq', 'head'), may hold values from -0.125 to 0.125
- conv_weight: bfloat16 [3, 4, 2048], P(None, None, 'head'), may hold values from -3 to 3
- forget_gap: bfloat16 [2048], P('head'), may hold values from 9.953976e-06 to 0.099609375
- gain_out: bfloat16 [2048], P('head'), may hold values from 0.5 to 1.5
- w_o: bfloat16 [2048, 2048], P('head', 'seq'), may hold values from -0.125 to 0.125
- gain_attn: bfloat16 [2048], P('head'), may hold values from 0.5 to 1.5
- gain_ffn: bfloat16 [2048], P('head'), may hold values from 0.5 to 1.5
- w_gate: bfloat16 [2048, 5632], P('seq', 'head'), may hold values from -0.125 to 0.125
- w_up: bfloat16 [2048, 5632], P('seq', 'head'), may hold values from -0.125 to 0.125
- w_down: bfloat16 [5632, 2048], P('head', 'seq'), may hold values from -0.078125 to 0.078125
- out_grad: bfloat16 [2, 8192, 2048], P(None, 'seq', 'head'), may hold values from -6 to 6
Outputs:
- output: bfloat16 [2, 8192, 2048], P(None, 'seq', 'head')
- input_grad: bfloat16 [2, 8192, 2048], P(None, 'seq', 'head')
- grad_w_q: float32 [2048, 2048], P('seq', 'head')
- grad_w_f: float32 [2048, 2048], P('seq', 'head')
- grad_w_i: float32 [2048, 2048], P('seq', 'head')
- grad_conv: float32 [3, 4, 2048], P(None, None, 'head')
- grad_forget_gap: float32 [2048], P('head')
- grad_gain_out: float32 [2048], P('head')
- grad_w_o: float32 [2048, 2048], P('head', 'seq')
- grad_gain_attn: float32 [2048], P('head')
- grad_gain_ffn: float32 [2048], P('head')
- grad_w_gate: float32 [2048, 5632], P('seq', 'head')
- grad_w_up: float32 [2048, 5632], P('seq', 'head')
- grad_w_down: float32 [5632, 2048], P('head', 'seq')
The draws below stay inside these ranges and needn't reach their ends.
All inputs are finite; a program needn't handle non-finite values.
Results may differ from the reference program's by a relative error of at most 0.017.
Values may be sent and summed in bfloat16 or wider, within the bound.
No kernel may reach another device: no remote copies, remote signals or barrier semaphores. Data moves between devices by JAX's collectives and lax.ppermute only.
A program may use at most 320 MiB of HBM per device.

```python
import math
import jax
import jax.numpy as jnp
from jax import lax

D = 2048
HEAD_DIM = 128
FF = 5632
KER = 4
SPAN = 128
MB = 2
LEN = 8192


def steps_of(stream_key, dims, shards, least, top_value):
    loudness, own = 1.0, jax.random.fold_in(stream_key, 6)
    for position, parts in shards:
        steps = jnp.exp(jax.random.uniform(jax.random.fold_in(own, position), (parts,), jnp.float32, least / len(shards), top_value / len(shards)))
        loudness = loudness * jnp.repeat(steps, dims[position] // parts).reshape([-1 if axis == position else 1 for axis in range(len(dims))])
    return loudness


def bell_draw(rng, extent, spread, bound, cuts=(), held_as=jnp.bfloat16):
    array = spread * jax.random.normal(rng, extent, jnp.float32)
    if cuts:
        array = array * steps_of(rng, extent, cuts, -0.22, 0.18)
    return jnp.clip(array, -bound, bound).astype(held_as)


def setup_inputs(seed: int = 0) -> dict:
    splits = jax.random.split(jax.random.key(seed), 15)
    return {
        "layer_input": bell_draw(splits[0], (MB, LEN, D), 1.0, 6.0, ((1, 64), (2, 2))),
        "w_q": bell_draw(splits[1], (D, D), D ** -0.5, 0.125, ((0, 64), (1, 2))),
        "w_f": bell_draw(splits[2], (D, D), D ** -0.5, 0.125, ((0, 64), (1, 2))),
        "w_i": bell_draw(splits[3], (D, D), D ** -0.5, 0.125, ((0, 64), (1, 2))),
        "conv_weight": bell_draw(splits[4], (3, KER, D), KER ** -0.5, 3.0, ((2, 2),)),
        "forget_gap": jnp.clip(jnp.exp(math.log(0.099609375) - 9.21104 * jax.random.uniform(splits[5], (D,), jnp.float32) ** steps_of(splits[5], (D,), ((0, 2),), -0.2, 0.2)), 9.953975677490234e-06, 0.099609375).astype(jnp.bfloat16),
        "gain_out": jnp.clip(1.0 + 0.1 * jax.random.normal(splits[6], (D,), jnp.float32), 0.5, 1.5).astype(jnp.bfloat16),
        "w_o": bell_draw(splits[7], (D, D), D ** -0.5, 0.125, ((0, 2), (1, 64))),
        "gain_attn": jnp.clip(1.0 + 0.1 * jax.random.normal(splits[8], (D,), jnp.float32), 0.5, 1.5).astype(jnp.bfloat16),
        "gain_ffn": jnp.clip(1.0 + 0.1 * jax.random.normal(splits[9], (D,), jnp.float32), 0.5, 1.5).astype(jnp.bfloat16),
        "w_gate": bell_draw(splits[10], (D, FF), D ** -0.5, 0.125, ((0, 64), (1, 2))),
        "w_up": bell_draw(splits[11], (D, FF), D ** -0.5, 0.125, ((0, 64), (1, 2))),
        "w_down": bell_draw(splits[12], (FF, D), FF ** -0.5, 0.078125, ((0, 2), (1, 64))),
        "out_grad": bell_draw(splits[13], (MB, LEN, D), 1.0, 6.0, ((1, 64), (2, 2))),
    }


norm_eps = 1e-06
highest = lax.Precision.HIGHEST

@jax.custom_vjp
def low(v):
    return lax.optimization_barrier(v.astype(jnp.bfloat16)).astype(jnp.float32)

@jax.custom_vjp
def low_back(v):
    return v

def low_keep(v):
    return (low(v), None)

def low_pass(kept, grad):
    return (grad,)

def back_keep(v):
    return (v, None)

def back_low(kept, grad):
    return (low(grad),)
low.defvjp(low_keep, low_pass)
low_back.defvjp(back_keep, back_low)

def matmul(a, b):
    return jnp.dot(a, b, precision=highest)

def rms_norm(v, gain):
    return v * lax.rsqrt(lax.optimization_barrier(jnp.mean(v * v, axis=-1, keepdims=True)) + norm_eps) * gain

def out_norm(mixer_out, values, gain):
    shaped = mixer_out.reshape(mixer_out.shape[:-1] + (-1, HEAD_DIM))
    scaled = shaped * lax.rsqrt(lax.optimization_barrier(jnp.mean(shaped * shaped, axis=-1, keepdims=True)) + norm_eps)
    return scaled.reshape(mixer_out.shape) * gain * jax.nn.silu(values)

def activate(q_conv, f_conv, i_conv, forget_gap):
    queries = jax.nn.silu(q_conv)
    key_in = forget_gap * jax.nn.sigmoid(-f_conv)
    log_decay = jnp.log1p(-key_in)
    return (queries, key_in, i_conv, log_decay)

def span_step(carried, pieces):
    memory, running = carried
    queries, key_in, values, log_decay = pieces
    cumulative = jnp.cumsum(log_decay, axis=-2)
    q_dec = queries * jnp.exp(cumulative)
    k_dec = key_in * jnp.exp(-cumulative)
    scores = jnp.einsum('...tk,...sk->...ts', q_dec, k_dec, precision=highest)
    length = queries.shape[-2]
    causal = jnp.arange(length)[:, None] >= jnp.arange(length)[None, :]
    scores = jnp.where(causal, scores, 0.0)
    outputs = jnp.einsum('...ts,...sv->...tv', scores, values, precision=highest)
    outputs = outputs + jnp.einsum('...tk,...kv->...tv', q_dec, memory, precision=highest)
    last_log = cumulative[..., -1, :]
    k_last = key_in * jnp.exp(last_log[..., None, :] - cumulative)
    memory = jnp.exp(last_log)[..., :, None] * memory + jnp.einsum('...sk,...sv->...kv', k_last, values, precision=highest)
    q_total = q_dec * jnp.exp(running)[..., None, :]
    return ((memory, running + last_log), (outputs, q_total))

def local_states(queries, key_in, values, log_decay):
    batches, length, channels = queries.shape
    head_count = channels // HEAD_DIM
    block_count = length // SPAN

    def to_blocks(v):
        return v.reshape(batches, block_count, SPAN, head_count, HEAD_DIM).transpose(1, 0, 3, 2, 4)

    def from_blocks(v):
        return v.transpose(1, 0, 3, 2, 4).reshape(batches, length, channels)
    initial = (jnp.zeros((batches, head_count, HEAD_DIM, HEAD_DIM), jnp.float32), jnp.zeros((batches, head_count, HEAD_DIM), jnp.float32))
    carried, stacked = lax.scan(jax.checkpoint(span_step), initial, (to_blocks(queries), to_blocks(key_in), to_blocks(values), to_blocks(log_decay)))
    return (from_blocks(stacked[0]), from_blocks(stacked[1]), carried[0], jnp.exp(carried[1]))

def short_conv(v, kernel):
    length = v.shape[0]
    padded = jnp.pad(v, ((KER - 1, 0), (0, 0)))
    result = kernel[0] * padded[0:length]
    for offset in range(1, KER):
        result = result + kernel[offset] * padded[offset:offset + length]
    return result

def block_layer(source, w_q, w_f, w_i, conv_weight, forget_gap, gain_out, w_o, gain_attn, gain_ffn, w_gate, w_up, w_down):
    normed = low(rms_norm(source, gain_attn))
    q_proj = low_back(low(matmul(normed, w_q)))
    f_proj = low_back(low(matmul(normed, w_f)))
    i_proj = low_back(low(matmul(normed, w_i)))
    q_conv = short_conv(q_proj, conv_weight[0])
    f_conv = short_conv(f_proj, conv_weight[1])
    i_conv = short_conv(i_proj, conv_weight[2])
    queries, key_in, values, log_decay = activate(q_conv, f_conv, i_conv, forget_gap)
    mixer_out = local_states(queries[None], key_in[None], values[None], log_decay[None])[0][0]
    gated = low(out_norm(mixer_out, values, gain_out))
    resid = source + low_back(matmul(gated, w_o))
    normed2 = low(rms_norm(resid, gain_ffn))
    gate_pre = low_back(matmul(normed2, w_gate))
    up_pre = low_back(matmul(normed2, w_up))
    hidden = low(jax.nn.silu(gate_pre) * up_pre)
    return resid + low_back(matmul(hidden, w_down))

def reference(layer_input, w_q, w_f, w_i, conv_weight, forget_gap, gain_out, w_o, gain_attn, gain_ffn, w_gate, w_up, w_down, out_grad):
    weights_f32 = tuple((p.astype(jnp.float32) for p in (w_q, w_f, w_i, conv_weight, forget_gap, gain_out, w_o, gain_attn, gain_ffn, w_gate, w_up, w_down)))

    def per_sequence(gradients, inputs_pair):
        source, cotangent = inputs_pair
        result, pullback = jax.vjp(block_layer, source.astype(jnp.float32), *weights_f32)
        pulled = pullback(cotangent.astype(jnp.float32))
        gradients = tuple((g + b for g, b in zip(gradients, pulled[1:])))
        return (gradients, (result.astype(jnp.bfloat16), pulled[0].astype(jnp.bfloat16)))
    initial = tuple((jnp.zeros_like(p) for p in weights_f32))
    gradients, outputs = lax.scan(per_sequence, initial, (layer_input, out_grad))
    return (outputs[0], outputs[1], gradients[0], gradients[1], gradients[2], gradients[3], gradients[4], gradients[5], gradients[6], gradients[7], gradients[8], gradients[9], gradients[10], gradients[11])
```

```python
import jax
import jax.numpy as jnp
from jax import lax
from jax.sharding import Mesh
from jax.sharding import PartitionSpec as P

HEAD_DIM = 128
KER = 4
SPAN = 128
RING = 4
PLANE = ("x", "z")
SEQ = ("x", "z", "y")

norm_eps = 1e-06
highest = lax.Precision.HIGHEST
f32 = jnp.float32
bf16 = jnp.bfloat16


def swap(block):
    return lax.ppermute(block, "head", [(0, 1), (1, 0)])


def exchange(block, axis):
    return lax.all_to_all(block, axis, 0, 0, tiled=True)


def gather_y(block):
    return exchange(jnp.broadcast_to(block[None], (RING,) + block.shape), "y")


def scatter_y(blocks):
    return jnp.sum(exchange(blocks, "y").astype(f32), axis=0)


def dot(a, b, contract):
    return lax.dot_general(a, b, (contract, ((), ())), preferred_element_type=f32)


def to_sequence(block, head):
    mine = lax.dynamic_index_in_dim(block, head, 0, False)
    other = swap(lax.dynamic_index_in_dim(block, 1 - head, 0, False))
    first = head == 0
    return jnp.concatenate((jnp.where(first, mine, other), jnp.where(first, other, mine)), axis=1)


def from_sequence(block, head):
    half = block.shape[1] // 2
    mine = lax.dynamic_slice_in_dim(block, head * half, half, 1)
    other = swap(lax.dynamic_slice_in_dim(block, (1 - head) * half, half, 1))
    first = head == 0
    return jnp.stack((jnp.where(first, mine, other), jnp.where(first, other, mine)))


def rms_norm(v, gain):
    return v * lax.rsqrt(jnp.mean(v * v, axis=-1, keepdims=True) + norm_eps) * gain


def out_norm(mixer_out, values, gain):
    scaled = mixer_out * lax.rsqrt(jnp.mean(mixer_out * mixer_out, axis=-1, keepdims=True) + norm_eps)
    return scaled * gain * jax.nn.silu(values)


def activate(q_conv, f_conv, i_conv, forget_gap):
    queries = jax.nn.silu(q_conv)
    key_in = forget_gap * jax.nn.sigmoid(-f_conv)
    log_decay = jnp.log1p(-key_in)
    return (queries, key_in, i_conv, log_decay)


def ein(form, a, b):
    return jnp.einsum(form, a, b, precision=highest)


def group_prefix(decay, state, reverse):
    groups = lax.axis_size(PLANE)
    heads, keys, width = state.shape
    rows = keys // groups
    packed = jnp.concatenate(
        (
            state.reshape(heads, groups, rows, width),
            jnp.broadcast_to(decay.reshape(heads, groups, rows, 1), (heads, groups, rows, width)),
        ),
        axis=2,
    ).transpose(1, 0, 2, 3)
    held = exchange(packed, PLANE)
    states, decays = held[:, :, :rows], held[:, :, rows:]
    order = range(groups - 1, -1, -1) if reverse else range(groups)
    entering = [None] * groups
    running = jnp.zeros_like(states[0])
    for g in order:
        entering[g] = running
        running = states[g] + decays[g] * running
    back = exchange(jnp.stack(entering), PLANE)
    return back.transpose(1, 0, 2, 3).reshape(heads, keys, width)


def short_conv(extended, kernel, length):
    result = kernel[0] * extended[0:length]
    for offset in range(1, KER):
        result = result + kernel[offset] * extended[offset : offset + length]
    return result


def gather_rows(packed):
    held = exchange(packed, "y")
    held = held.reshape((RING * packed.shape[1],) + packed.shape[2:])
    return lax.all_gather(held, PLANE, axis=0, tiled=True)


def for_y(w):
    rows, columns = w.shape
    return w.reshape(rows, RING, columns // RING).transpose(1, 0, 2)


def body(
    layer_input,
    w_q,
    w_f,
    w_i,
    conv_weight,
    forget_gap,
    gain_out,
    w_o,
    gain_attn,
    gain_ffn,
    w_gate,
    w_up,
    w_down,
    out_grad,
):
    head = lax.axis_index("head")
    place = lax.axis_index("y")
    groups = lax.axis_size(PLANE)
    length = layer_input.shape[1]
    width = 2 * layer_input.shape[2]
    slice_width = w_q.shape[1] // RING
    ff_slice = w_gate.shape[1] // RING
    tokens = RING * length

    attn_packed = jnp.concatenate((for_y(w_q), for_y(w_f), for_y(w_i)), axis=2)
    proj_a = gather_rows(attn_packed)
    w_ot = w_o.T
    o_a = lax.all_gather(
        gather_y(w_ot).reshape(RING * w_ot.shape[0], w_ot.shape[1]), PLANE, axis=0, tiled=True
    )
    ff_packed = jnp.stack((for_y(w_gate), for_y(w_up), for_y(w_down.T)), axis=1)
    held = exchange(ff_packed, "y").transpose(1, 0, 2, 3).reshape(3, -1, ff_slice)
    ff_a = lax.all_gather(held, PLANE, axis=1, tiled=True)
    proj_b, o_b, ff_b = swap(proj_a), swap(o_a), swap(ff_a)

    def channel_slice(v):
        own = lax.dynamic_slice_in_dim(v, place * slice_width, slice_width, v.ndim - 1)
        return own

    small_own = jnp.concatenate(
        (
            channel_slice(conv_weight).reshape(3 * KER, slice_width),
            channel_slice(forget_gap)[None],
            channel_slice(gain_out)[None],
        )
    )
    small = jnp.concatenate((small_own, swap(small_own)), axis=1).astype(f32)
    heads = 2 * slice_width // HEAD_DIM
    conv_k = small[: 3 * KER].reshape(3, KER, 2 * slice_width)
    gap = small[3 * KER].reshape(heads, 1, 1, HEAD_DIM)
    gain_o = small[3 * KER + 1].reshape(heads, 1, 1, HEAD_DIM)
    gains_own = jnp.stack((gain_attn, gain_ffn))
    gains_other = swap(gains_own)
    gains = jnp.where(
        head == 0,
        jnp.concatenate((gains_own, gains_other), axis=1),
        jnp.concatenate((gains_other, gains_own), axis=1),
    ).astype(f32)
    g_attn, g_ffn = gains[0], gains[1]

    x_own = to_sequence(layer_input, head)
    dy_own = to_sequence(out_grad, head)
    x_all = gather_y(x_own).reshape(tokens, width).astype(f32)
    dy_all = gather_y(dy_own).reshape(tokens, width)
    normed = rms_norm(x_all, g_attn).astype(bf16)

    c_rows = ((1,), (0,))
    c_cols = ((1,), (1,))
    c_toks = ((0,), (0,))
    projected = jnp.concatenate(
        [dot(normed, w, c_rows).astype(bf16).reshape(tokens, 3, slice_width) for w in (proj_a, proj_b)],
        axis=2,
    )
    route = [(i, i + 1) for i in range(groups - 1)]
    before = lax.ppermute(projected[tokens - (KER - 1) :], PLANE, route)
    extended = jnp.concatenate((before, projected)).astype(f32)
    taps = conv_k.transpose(1, 0, 2)
    conv_out, conv_pull = jax.vjp(lambda e, k: short_conv(e, k, tokens), extended, taps)

    def units(v):
        return v.reshape(RING, SPAN, heads, HEAD_DIM).transpose(2, 0, 1, 3)

    def from_units(v):
        return v.transpose(1, 2, 0, 3).reshape(tokens, heads * HEAD_DIM)

    (queries, key_in, values, log_decay), act_pull = jax.vjp(
        activate, units(conv_out[:, 0]), units(conv_out[:, 1]), units(conv_out[:, 2]), gap
    )
    cumulative = jnp.cumsum(log_decay, axis=-2)
    last_log = cumulative[..., -1:, :]
    grow = jnp.exp(cumulative)
    shrink = jnp.exp(-cumulative)
    rest = jnp.exp(last_log - cumulative)
    q_dec = queries * grow
    k_dec = key_in * shrink
    k_last = key_in * rest
    block_decay = jnp.exp(last_log[..., 0, :])
    causal = jnp.arange(SPAN)[:, None] >= jnp.arange(SPAN)[None, :]
    added = ein("hnsk,hnsv->hnkv", k_last, values)
    local = jnp.zeros_like(added[:, 0])
    for n in range(RING):
        local = added[:, n] + block_decay[:, n, :, None] * local
    group_decay = jnp.prod(block_decay, axis=1)
    state = group_prefix(group_decay, local, False)
    scores = jnp.where(causal, ein("hntk,hnsk->hnts", q_dec, k_dec), 0.0)
    intra = ein("hnts,hnsv->hntv", scores, values)
    entering = []
    for n in range(RING):
        entering.append(state)
        state = added[:, n] + block_decay[:, n, :, None] * state
    entering = jnp.stack(entering, axis=1)
    mixer_out = intra + ein("hntk,hnkv->hntv", q_dec, entering)
    gated_f32, gate_norm_pull = jax.vjp(out_norm, mixer_out, values, gain_o)
    gated = from_units(gated_f32.astype(bf16))

    gathered = gather_y(gated).reshape(RING, tokens, 2, slice_width)

    def all_channels(half):
        return gathered[:, :, half].transpose(1, 0, 2).reshape(tokens, RING * slice_width)

    attn_sum = dot(all_channels(0), o_a, c_cols) + dot(all_channels(1), o_b, c_cols)
    resid = x_all + attn_sum
    normed2 = rms_norm(resid, g_ffn).astype(bf16)

    ffn_part = 0.0
    grad_normed2 = 0.0
    ff_grads = []
    for ff in (ff_a, ff_b):
        gate_w, up_w, down_t = ff[0], ff[1], ff[2]
        grad_hidden = dot(dy_all, down_t, c_rows)
        gate_pre = dot(normed2, gate_w, c_rows)
        up_pre = dot(normed2, up_w, c_rows)
        sig = jax.nn.sigmoid(gate_pre)
        silu_gate = gate_pre * sig
        hidden = (silu_gate * up_pre).astype(bf16)
        grad_gate = (grad_hidden * up_pre * (sig * (1.0 + gate_pre * (1.0 - sig)))).astype(bf16)
        grad_up = (grad_hidden * silu_gate).astype(bf16)
        grad_normed2 = grad_normed2 + dot(grad_gate, gate_w, c_cols) + dot(grad_up, up_w, c_cols)
        ffn_part = ffn_part + dot(hidden, down_t, c_cols)
        ff_grads.append(
            jnp.stack(
                [
                    dot(a, b, c_toks).astype(bf16)
                    for a, b in ((normed2, grad_gate), (normed2, grad_up), (dy_all, hidden))
                ]
            )
        )

    def split_tokens(v):
        return v.astype(bf16).reshape(RING, length, width)

    def own_tokens(v):
        return lax.dynamic_slice_in_dim(v, place * length, length, 0)

    resid_own = own_tokens(resid)
    grad_normed2 = scatter_y(split_tokens(grad_normed2))
    _, norm2_pull = jax.vjp(rms_norm, resid_own, g_ffn)
    grad_resid_norm, grad_g_ffn = norm2_pull(grad_normed2)
    grad_resid = dy_own.astype(f32) + grad_resid_norm
    grad_attn_own = grad_resid.astype(bf16)
    grad_attn = gather_y(grad_attn_own).reshape(tokens, width)

    output = (resid_own + scatter_y(split_tokens(ffn_part))).astype(bf16)
    output = from_sequence(output, head)

    def o_slice(w):
        return lax.dynamic_slice_in_dim(w, place * slice_width, slice_width, 1)

    grad_gated = jnp.concatenate([dot(grad_attn, o_slice(w), c_rows) for w in (o_a, o_b)], axis=1)
    grad_mixer, grad_values_gate, grad_gain_o = gate_norm_pull(units(grad_gated))
    added_back = ein("hntk,hntv->hnkv", q_dec, grad_mixer)
    local = jnp.zeros_like(added_back[:, 0])
    for n in range(RING - 1, -1, -1):
        local = added_back[:, n] + block_decay[:, n, :, None] * local
    grad_state = group_prefix(group_decay, local, True)
    leaving = [None] * RING
    for n in range(RING - 1, -1, -1):
        leaving[n] = grad_state
        grad_state = added_back[:, n] + block_decay[:, n, :, None] * grad_state
    leaving = jnp.stack(leaving, axis=1)
    grad_scores = jnp.where(causal, ein("hntv,hnsv->hnts", grad_mixer, values), 0.0)
    grad_q_dec = ein("hnts,hnsk->hntk", grad_scores, k_dec) + ein("hntv,hnkv->hntk", grad_mixer, entering)
    grad_k_dec = ein("hnts,hntk->hnsk", grad_scores, q_dec)
    grad_values = ein("hnts,hntv->hnsv", scores, grad_mixer) + ein("hnsk,hnkv->hnsv", k_last, leaving)
    grad_k_last = ein("hnsv,hnkv->hnsk", values, leaving)
    grad_block_decay = jnp.sum(entering * leaving, axis=-1)
    through_last = grad_k_last * k_last
    grad_cumulative = grad_q_dec * q_dec - grad_k_dec * k_dec - through_last
    grad_last = jnp.sum(through_last, axis=-2) + grad_block_decay * block_decay
    grad_log = lax.cumsum(grad_cumulative, axis=2, reverse=True) + grad_last[:, :, None, :]
    grad_queries = grad_q_dec * grow
    grad_key = grad_k_dec * shrink + grad_k_last * rest
    grad_q, grad_f, grad_i, grad_gap = act_pull(
        (grad_queries, grad_key, grad_values + grad_values_gate, grad_log)
    )
    grad_conv_out = jnp.stack([from_units(v) for v in (grad_q, grad_f, grad_i)], axis=1)
    grad_extended, grad_taps = conv_pull(grad_conv_out)
    route = [(i + 1, i) for i in range(groups - 1)]
    sent_back = lax.ppermute(grad_extended[: KER - 1].astype(bf16), PLANE, route).astype(f32)
    grad_own = grad_extended[KER - 1 :]
    grad_proj = jnp.concatenate(
        (grad_own[: tokens - (KER - 1)], grad_own[tokens - (KER - 1) :] + sent_back)
    ).astype(bf16)
    grad_proj_a = grad_proj[:, :, :slice_width].reshape(tokens, 3 * slice_width)
    grad_proj_b = grad_proj[:, :, slice_width:].reshape(tokens, 3 * slice_width)
    grad_normed = dot(grad_proj_a, proj_a, c_cols) + dot(grad_proj_b, proj_b, c_cols)
    grad_normed = scatter_y(split_tokens(grad_normed))
    _, norm1_pull = jax.vjp(rms_norm, x_own.astype(f32), g_attn)
    grad_x_norm, grad_g_attn = norm1_pull(grad_normed)
    input_grad = from_sequence((grad_resid + grad_x_norm).astype(bf16), head)

    def both(own, other):
        return (own.astype(f32) + swap(other).astype(f32)).astype(bf16)

    ff_sum = both(*ff_grads)
    ff_sum = ff_sum.reshape(3, groups, -1, ff_slice).transpose(1, 0, 2, 3)
    ff_sum = lax.psum_scatter(ff_sum, PLANE, scatter_dimension=0, tiled=True)[0]
    ff_sum = ff_sum.reshape(3, RING, -1, ff_slice).transpose(1, 0, 2, 3)
    ff_sum = exchange(ff_sum, "y").astype(f32)

    grad_o_a = dot(grad_attn, gated[:, :slice_width], c_toks).astype(bf16)
    grad_o_b = dot(grad_attn, gated[:, slice_width:], c_toks).astype(bf16)
    attn_grad = both(
        jnp.concatenate((dot(normed, grad_proj_a, c_toks).astype(bf16), grad_o_a), axis=1),
        jnp.concatenate((dot(normed, grad_proj_b, c_toks).astype(bf16), grad_o_b), axis=1),
    )
    attn_sum = lax.psum_scatter(attn_grad, PLANE, scatter_dimension=0, tiled=True)
    attn_sum = exchange(attn_sum.reshape(RING, -1, 4 * slice_width), "y").astype(f32)

    def columns(v):
        return v.transpose(1, 0, 2).reshape(v.shape[1], -1)

    def turned(v):
        return v.transpose(0, 2, 1).reshape(-1, v.shape[1])

    grads = [columns(attn_sum[..., j * slice_width : (j + 1) * slice_width]) for j in range(3)]
    grad_w_o = turned(attn_sum[..., 3 * slice_width :])
    grad_w_gate, grad_w_up = columns(ff_sum[:, 0]), columns(ff_sum[:, 1])
    grad_w_down = turned(ff_sum[:, 2])

    per_channel = jnp.concatenate(
        (
            grad_taps.transpose(1, 0, 2).reshape(3 * KER, -1),
            grad_gap.reshape(1, -1),
            grad_gain_o.reshape(1, -1),
        )
    )
    per_feature = jnp.stack((grad_g_attn, grad_g_ffn))
    half = width // 2
    own = lax.dynamic_slice_in_dim(per_feature, head * half, half, 1)
    other = lax.dynamic_slice_in_dim(per_feature, (1 - head) * half, half, 1)

    def spread(v, rest):
        return jnp.concatenate(
            (lax.dynamic_update_slice(jnp.zeros((v.shape[0], half), f32), v, (0, place * slice_width)), rest)
        )

    small_grad = spread(per_channel[:, :slice_width], own) + swap(spread(per_channel[:, slice_width:], other))
    rows = small_grad.shape[0]
    count = lax.axis_size(SEQ)
    part = jnp.sum(exchange(small_grad.reshape(count, -1, 128), SEQ).reshape(count, -1), axis=0)
    part = jnp.broadcast_to(part.reshape(1, -1, 128), (count, part.shape[0] // 128, 128))
    small_grad = exchange(part, SEQ).reshape(rows, half)
    return (
        output,
        input_grad,
        grads[0],
        grads[1],
        grads[2],
        small_grad[: 3 * KER].reshape(3, KER, half),
        small_grad[3 * KER],
        small_grad[3 * KER + 1],
        grad_w_o,
        small_grad[3 * KER + 2],
        small_grad[3 * KER + 3],
        grad_w_gate,
        grad_w_up,
        grad_w_down,
    )


def solution(mesh):
    fine = Mesh(mesh.devices.reshape(4, 4, RING, 2), ("x", "z", "y", "head"))
    tokens = P(None, SEQ, "head")
    rows = P(SEQ, "head")
    columns = P("head", SEQ)
    channels = P("head")
    taps = P(None, None, "head")
    return jax.shard_map(
        body,
        mesh=fine,
        in_specs=(
            tokens,
            rows,
            rows,
            rows,
            taps,
            channels,
            channels,
            columns,
            channels,
            channels,
            rows,
            rows,
            columns,
            tokens,
        ),
        out_specs=(
            tokens,
            tokens,
            rows,
            rows,
            rows,
            taps,
            channels,
            channels,
            columns,
            channels,
            channels,
            rows,
            rows,
            columns,
        ),
        check_vma=False,
    )
```

```python
import functools

import jax
import jax.numpy as jnp
from jax import lax
from jax.experimental import pallas as pl
from jax.experimental.pallas import tpu as pltpu
from jax.sharding import Mesh
from jax.sharding import PartitionSpec as P

HEAD_DIM = 128
KER = 4
SPAN = 128
RING = 4
EDGE = 16
PLANE = ("x", "z")
SEQ = ("x", "z", "y")

norm_eps = 1e-06
f32 = jnp.float32
bf16 = jnp.bfloat16
MIB = 1 << 20

c_rows = (((1,), (0,)), ((), ()))
c_cols = (((1,), (1,)), ((), ()))
c_toks = (((0,), (0,)), ((), ()))


def swap(block):
    return lax.ppermute(block, "head", [(0, 1), (1, 0)])


def exchange(block, axis):
    return lax.all_to_all(block, axis, 0, 0, tiled=True)


def from_ring(block, r):
    return lax.ppermute(block, "y", [((i + r) % RING, i) for i in range(RING)])


def ring_gather(block):
    return [block] + [from_ring(block, r) for r in range(1, RING)]


def ring_scatter(parts):
    return [parts[0]] + [from_ring(parts[r], RING - r) for r in range(1, RING)]


def ring_exchange(parts, place):
    sent = [lax.dynamic_index_in_dim(parts, (place - r) % RING, 0, False) for r in range(RING)]
    got = [sent[0]] + [from_ring(sent[r], r) for r in range(1, RING)]
    return lax.dynamic_slice_in_dim(jnp.stack(got + got), (RING - place) % RING, RING, 0)


def axis_sum(v, axis):
    count = lax.axis_size(axis)
    others = [lax.ppermute(v, axis, [((i + r) % count, i) for i in range(count)]) for r in range(1, count)]
    return sum(others, v)


def half_of(at_ref, k):
    return lax.rem(at_ref[1] + k, 2)


def slot(place_ref, r):
    return pl.ds(pl.multiple_of(lax.rem(place_ref[0] + r, RING) * SPAN, SPAN), SPAN)


def mm(a, b, contract):
    return lax.dot_general(a.astype(bf16), b.astype(bf16), contract, preferred_element_type=f32)


def ones_dot(ones, v, contract):
    high = v.astype(bf16)
    rest = v - high.astype(f32)
    middle = rest.astype(bf16)
    low = (rest - middle.astype(f32)).astype(bf16)
    return sum(
        lax.dot_general(ones, part, contract, preferred_element_type=f32) for part in (low, middle, high)
    )


def kernel_call(body, out_shape, grid, in_specs, out_specs, scratch=(), vmem=56, prefetch=0):
    return pl.pallas_call(
        body,
        out_shape=out_shape,
        grid_spec=pltpu.PrefetchScalarGridSpec(
            num_scalar_prefetch=prefetch,
            grid=grid,
            in_specs=in_specs,
            out_specs=out_specs,
            scratch_shapes=list(scratch),
        ),
        compiler_params=pltpu.CompilerParams(vmem_limit_bytes=vmem * MIB),
        cost_estimate=pl.CostEstimate(flops=1000, bytes_accessed=1000, transcendentals=0),
    )


def shape(dims, dtype):
    return jax.ShapeDtypeStruct(tuple(dims), dtype)


def whole(dims):
    return pl.BlockSpec(tuple(dims), lambda *_: (0,) * len(dims))


def sigmoid(v):
    return 1.0 / (1.0 + jnp.exp(-v))


def triangle(lower):
    row = lax.broadcasted_iota(jnp.int32, (SPAN, SPAN), 0)
    col = lax.broadcasted_iota(jnp.int32, (SPAN, SPAN), 1)
    return row >= col if lower else row <= col


def project_kernel(place_ref, *refs):
    x_refs = refs[:RING]
    before_ref, g_ref, w_ref, normed_ref, edge_ref, proj_ref, halo_ref = refs[RING:]

    def norm(v):
        return (v * lax.rsqrt(jnp.mean(v * v, axis=-1, keepdims=True) + norm_eps) * g_ref[...]).astype(bf16)

    @pl.when(pl.program_id(0) == 0)
    def _():
        for r in range(RING):
            normed_ref[slot(place_ref, r), :] = norm(x_refs[r][...].astype(f32))
        edge_ref[...] = norm(before_ref[...].astype(f32))

    proj_ref[...] = mm(normed_ref[...], w_ref[...], c_rows).astype(bf16)
    halo_ref[...] = mm(edge_ref[...], w_ref[...], c_rows).astype(bf16)


def project(at, blocks, before, gain, w, columns):
    length, width = blocks[0].shape
    tokens = RING * length
    return kernel_call(
        project_kernel,
        (
            shape((tokens, width), bf16),
            shape((EDGE, width), bf16),
            shape((tokens, 2 * columns), bf16),
            shape((EDGE, 2 * columns), bf16),
        ),
        (2,),
        [whole(blocks[0].shape)] * RING
        + [
            whole(before.shape),
            whole(gain.shape),
            pl.BlockSpec((None, width, columns), lambda i, p: (half_of(p, i), 0, 0)),
        ],
        [
            whole((tokens, width)),
            whole((EDGE, width)),
            pl.BlockSpec((tokens, columns), lambda i, _: (0, i)),
            pl.BlockSpec((EDGE, columns), lambda i, _: (0, i)),
        ],
        prefetch=1,
    )(at, *blocks, before, gain, w)


def project_more_kernel(at_ref, n_ref, edge_ref, wa_ref, wb_ref, proj_ref, halo_ref):
    columns = wa_ref.shape[1]
    for k, w_ref in enumerate((wa_ref, wb_ref)):
        at = slice(k * columns, (k + 1) * columns)
        proj_ref[:, at] = mm(n_ref[...], w_ref[...], c_rows).astype(bf16)
        halo_ref[:, at] = mm(edge_ref[...], w_ref[...], c_rows).astype(bf16)


def project_more(at, normed, edge, w, columns):
    tokens, width = normed.shape
    last = w.shape[2] // columns - 1
    dims = ((tokens, 2 * columns), (EDGE, 2 * columns))
    return kernel_call(
        project_more_kernel,
        tuple(shape(d, bf16) for d in dims),
        (1,),
        [whole(normed.shape), whole(edge.shape)]
        + [pl.BlockSpec((None, width, columns), lambda i, p, k=k: (half_of(p, k), 0, last)) for k in range(2)],
        [whole(d) for d in dims],
        prefetch=1,
    )(at, normed, edge, w, w)


def assemble_kernel(place_ref, *refs):
    for r in range(RING):
        refs[-1][slot(place_ref, r), :] = refs[r][...]


def assemble(place, blocks):
    length, width = blocks[0].shape
    return kernel_call(
        assemble_kernel,
        shape((RING * length, width), blocks[0].dtype),
        (1,),
        [whole(blocks[0].shape)] * RING,
        whole((RING * length, width)),
        vmem=16,
        prefetch=1,
    )(place, *blocks)


def place_of(branch):
    if branch == 0:
        return lambda h: (0, h)
    return lambda h: (0, (h // 2) * 4 + (branch - 1) * 2 + h % 2)


def conv_of(ext, proj_ref, halo_ref, taps_ref, branch, tokens):
    ext[0:EDGE, :] = halo_ref[...].astype(f32)
    ext[EDGE:, :] = proj_ref[...].astype(f32)
    first = EDGE - (KER - 1)
    total = taps_ref[branch * KER, :][None] * ext[first : first + tokens, :]
    for j in range(1, KER):
        tap = taps_ref[branch * KER + j, :][None]
        total = total + tap * ext[first + j : first + j + tokens, :]
    return total


def spread_out(row):
    return jnp.transpose(jnp.broadcast_to(row, (HEAD_DIM, HEAD_DIM)))


def local_kernel(pf, pi, hf, hi, taps_ref, fc_ref, v_ref, cum_ref, kd_ref, added_ref, decay_ref, packed_ref, ext):
    tokens = pf.shape[0]
    fc_ref[...] = conv_of(ext, pf, hf, taps_ref, 1, tokens)
    v_ref[...] = conv_of(ext, pi, hi, taps_ref, 2, tokens)
    gap = taps_ref[3 * KER, :][None]
    tril = jnp.where(triangle(True), 1.0, 0.0).astype(bf16)
    state = jnp.zeros((HEAD_DIM, HEAD_DIM), f32)
    group = jnp.ones((HEAD_DIM, HEAD_DIM), f32)
    for n in range(tokens // SPAN):
        rows = pl.ds(n * SPAN, SPAN)
        f, v = fc_ref[rows, :], v_ref[rows, :]
        key = gap * sigmoid(-f)
        cum = ones_dot(tril, jnp.log1p(-key), c_rows)
        last = cum[SPAN - 1 :, :]
        decay = spread_out(jnp.exp(last))
        added = mm(key * jnp.exp(last - cum), v, c_toks)
        cum_ref[rows, :] = cum
        kd_ref[rows, :] = (key * jnp.exp(-cum)).astype(bf16)
        added_ref[0, n] = added
        decay_ref[0, n] = decay
        state = added + decay * state
        group = group * decay
    parts = packed_ref.shape[0]
    keys = HEAD_DIM // parts
    packed_ref[:, 0, :keys, :] = state.reshape(parts, keys, HEAD_DIM)
    packed_ref[:, 0, keys:, :] = group.reshape(parts, keys, HEAD_DIM)


def per_head(tokens):
    return pl.BlockSpec((tokens, HEAD_DIM), lambda h: (0, h))


def per_unit(blocks):
    return pl.BlockSpec((1, blocks, HEAD_DIM, HEAD_DIM), lambda h: (h, 0, 0, 0))


def local_part(proj, halo, taps, heads, groups):
    tokens = proj.shape[0]
    blocks = tokens // SPAN
    flat = (tokens, heads * HEAD_DIM)
    units = (heads, blocks, HEAD_DIM, HEAD_DIM)
    keys = HEAD_DIM // groups
    packed = (groups, heads, 2 * keys, HEAD_DIM)
    return kernel_call(
        local_kernel,
        (
            *(shape(flat, f32) for _ in range(3)),
            shape(flat, bf16),
            shape(units, f32),
            shape(units, f32),
            shape(packed, f32),
        ),
        (heads,),
        [pl.BlockSpec((tokens, HEAD_DIM), place_of(k)) for k in (1, 2)]
        + [pl.BlockSpec((EDGE, HEAD_DIM), place_of(k)) for k in (1, 2)]
        + [pl.BlockSpec((taps.shape[0], HEAD_DIM), lambda h: (0, h))],
        [per_head(tokens)] * 4
        + [per_unit(blocks)] * 2
        + [pl.BlockSpec((groups, 1, 2 * keys, HEAD_DIM), lambda h: (0, h, 0, 0))],
        scratch=[pltpu.VMEM((tokens + EDGE, HEAD_DIM), f32)],
    )(proj, proj, halo, halo, taps)


def query_kernel(pq, hq, taps_ref, v_ref, cum_ref, kd_ref, qc_ref, qd_ref, intra_ref, ext):
    tokens = pq.shape[0]
    qc_ref[...] = conv_of(ext, pq, hq, taps_ref, 0, tokens)
    lower = triangle(True)
    for n in range(tokens // SPAN):
        rows = pl.ds(n * SPAN, SPAN)
        q = qc_ref[rows, :]
        q_dec = (q * sigmoid(q) * jnp.exp(cum_ref[rows, :])).astype(bf16)
        scores = jnp.where(lower, mm(q_dec, kd_ref[rows, :], c_cols), 0.0)
        intra_ref[rows, :] = mm(scores, v_ref[rows, :], c_rows)
        qd_ref[rows, :] = q_dec


def query_part(proj, halo, taps, v, cum, kd):
    tokens, channels = v.shape
    return kernel_call(
        query_kernel,
        (shape(v.shape, f32), shape(v.shape, bf16), shape(v.shape, f32)),
        (channels // HEAD_DIM,),
        [per_head(tokens), per_head(EDGE), per_head(taps.shape[0])] + [per_head(tokens)] * 3,
        [per_head(tokens)] * 3,
        scratch=[pltpu.VMEM((tokens + EDGE, HEAD_DIM), f32)],
    )(proj, halo, taps, v, cum, kd)


def scan_kernel(reverse, held_ref, out_ref):
    groups, _, keys, _ = out_ref.shape
    state = jnp.zeros(out_ref.shape[1:], f32)
    for g in range(groups - 1, -1, -1) if reverse else range(groups):
        out_ref[g] = state
        state = held_ref[g, :, :keys, :] + held_ref[g, :, keys:, :] * state


def scan_states(held, reverse):
    groups, heads, double, width = held.shape
    dims = (groups, heads, double // 2, width)
    return kernel_call(
        functools.partial(scan_kernel, reverse),
        shape(dims, f32),
        (1,),
        [whole(held.shape)],
        whole(dims),
        vmem=16,
    )(held)


def mix_kernel(qd_ref, v_ref, intra_ref, added_ref, decay_ref, state_ref, taps_ref, gated_ref, mixed_ref, enter_ref):
    state = state_ref[...].reshape(HEAD_DIM, HEAD_DIM)
    gain = taps_ref[3 * KER + 1, :][None]
    for n in range(qd_ref.shape[0] // SPAN):
        rows = pl.ds(n * SPAN, SPAN)
        enter_ref[0, n] = state
        mixed = intra_ref[rows, :] + mm(qd_ref[rows, :], state, c_rows)
        state = added_ref[0, n] + decay_ref[0, n] * state
        mixed_ref[rows, :] = mixed
        v = v_ref[rows, :]
        scale = lax.rsqrt(jnp.mean(mixed * mixed, axis=-1, keepdims=True) + norm_eps)
        gated = (mixed * scale * gain * (v * sigmoid(v))).astype(bf16)
        for r in range(RING):
            gated_ref[r, rows, :] = gated


def mix(qd, v, intra, added, decay, state, taps):
    tokens, channels = qd.shape
    heads, blocks = added.shape[:2]
    return kernel_call(
        mix_kernel,
        (
            shape((RING, tokens, channels), bf16),
            shape((tokens, channels), f32),
            shape(added.shape, f32),
        ),
        (heads,),
        [per_head(tokens)] * 3
        + [per_unit(blocks)] * 2
        + [
            pl.BlockSpec((state.shape[0], 1) + state.shape[2:], lambda h: (0, h, 0, 0)),
            pl.BlockSpec((taps.shape[0], HEAD_DIM), lambda h: (0, h)),
        ],
        [
            pl.BlockSpec((RING, tokens, HEAD_DIM), lambda h: (0, 0, h)),
            per_head(tokens),
            per_unit(blocks),
        ],
    )(qd, v, intra, added, decay, state, taps)


def attend_kernel(place_ref, gated_ref, *rest):
    wa_refs, wb_refs = rest[:RING], rest[RING : 2 * RING]
    x_refs = rest[2 * RING : 3 * RING]
    g_ref, normed_ref, resid_ref, held, squares = rest[3 * RING :]
    step = pl.program_id(0)
    part = gated_ref.shape[2] // 2
    tile = x_refs[0].shape[1]
    for r in range(RING):
        held[step, slot(place_ref, r), :] = x_refs[r][...].astype(f32)
    total = held[step]
    for s in range(RING):
        total = total + mm(gated_ref[s, :, :part], wa_refs[s][...], c_cols)
        total = total + mm(gated_ref[s, :, part:], wb_refs[s][...], c_cols)
    held[step] = total
    square = jnp.sum(total * total, axis=-1, keepdims=True)

    @pl.when(step == 0)
    def _():
        squares[...] = square

    @pl.when(step > 0)
    def _():
        squares[...] += square

    @pl.when(step == pl.num_programs(0) - 1)
    def _():
        steps = held.shape[0]
        scale = lax.rsqrt(squares[...] / (steps * tile) + norm_eps)
        length = resid_ref.shape[0]
        own = pl.ds(pl.multiple_of(place_ref[0] * length, length), length)
        for t in range(steps):
            columns = pl.ds(t * tile, tile)
            normed_ref[:, columns] = (held[t] * scale * g_ref[:, columns]).astype(bf16)
            resid_ref[:, columns] = held[t, own, :]


def attend(place, gathered, w, x, gain, tile=512):
    _, tokens, channels = gathered.shape
    part = channels // 2
    length, width = x[0].shape
    first = w.shape[2] // part - RING
    weights = [
        pl.BlockSpec((None, tile, part), lambda i, p, k=k, s=s: (half_of(p, k), i, first + s))
        for k in range(2)
        for s in range(RING)
    ]
    return kernel_call(
        attend_kernel,
        (shape((tokens, width), bf16), shape((length, width), f32)),
        (width // tile,),
        [whole(gathered.shape)]
        + weights
        + [pl.BlockSpec((length, tile), lambda i, _: (0, i))] * RING
        + [whole(gain.shape)],
        [whole((tokens, width)), whole((length, width))],
        scratch=[pltpu.VMEM((width // tile, tokens, tile), f32), pltpu.VMEM((tokens, 1), f32)],
        prefetch=1,
    )(place, gathered, *[w] * (2 * RING), *x, gain)


def units_kernel(at_ref, n_ref, dy_ref, gate_ref, up_ref, down_ref, *out_refs):
    gate = mm(n_ref[...], gate_ref[...], c_rows)
    up = mm(n_ref[...], up_ref[...], c_rows)
    grad = mm(dy_ref[...], down_ref[...], c_rows)
    sig = sigmoid(gate)
    silu = gate * sig
    results = (silu * up, grad * up * (sig * (1.0 + gate * (1.0 - sig))), grad * silu)
    steps = pl.num_programs(0) // 2
    for k, out_ref in enumerate(out_refs):

        @pl.when(pl.program_id(0) // steps == k)
        def _():
            for j, result in enumerate(results):
                out_ref[j] = result.astype(bf16)


def hidden_units(at, normed, dy, w, columns, tile=256):
    tokens, width = normed.shape
    steps = columns // tile
    return kernel_call(
        units_kernel,
        (shape((3, tokens, columns), bf16), shape((3, tokens, columns), bf16)),
        (2 * steps,),
        [whole(normed.shape), whole(dy.shape)]
        + [
            pl.BlockSpec(
                (None, width, tile), lambda i, p, k=k: (half_of(p, i // steps), 0, k * steps + i % steps)
            )
            for k in range(3)
        ],
        [
            pl.BlockSpec((3, tokens, tile), lambda i, _: (0, 0, jnp.minimum(i, steps - 1))),
            pl.BlockSpec((3, tokens, tile), lambda i, _: (0, 0, jnp.maximum(i - steps, 0))),
        ],
        prefetch=1,
    )(at, normed, dy, w, w, w)


def back_kernel(pairs, apart, at_ref, ua_ref, ub_ref, *refs):
    count = len(pairs)
    total = 0.0
    for k, u_ref in enumerate((ua_ref, ub_ref)):
        for (u, _), w_ref in zip(pairs, refs[k * count : (k + 1) * count]):
            total = total + mm(u_ref[u], w_ref[...], c_cols)
    if not apart:
        refs[-1][...] = total.astype(bf16)
        return
    held = refs[-1]
    held[...] = total.astype(bf16)
    for r in range(RING):
        refs[2 * count + r][...] = held[slot(at_ref, r), :]


def units_back(at, pairs, ua, ub, w, apart=False, tile=512):
    _, tokens, columns = ua.shape
    width = w.shape[1]
    count = RING if apart else 1
    rows = tokens // count
    outs = [shape((rows, width), bf16)] * count
    specs = [pl.BlockSpec((rows, tile), lambda i, _: (0, i))] * count
    return kernel_call(
        functools.partial(back_kernel, pairs, apart),
        tuple(outs) if apart else outs[0],
        (width // tile,),
        [whole(ua.shape), whole(ub.shape)]
        + [
            pl.BlockSpec((None, tile, columns), lambda i, p, k=k, c=c: (half_of(p, k), i, c))
            for k in range(2)
            for _, c in pairs
        ],
        specs if apart else specs[0],
        scratch=[pltpu.VMEM((tokens, tile), bf16)] if apart else [],
        prefetch=1,
    )(at, ua, ub, *[w] * (2 * len(pairs)))


def weight_grad_kernel(plan, lefts, *refs):
    mine, theirs = refs[2 * lefts : 2 * lefts + 2]
    out_ref = refs[-1]
    width = mine.shape[2]
    for j, (left, k) in enumerate(plan):
        grad = mm(refs[2 * left][...], mine[k], c_toks) + mm(refs[2 * left + 1][...], theirs[k], c_toks)
        out_ref[:, j * width : (j + 1) * width] = grad.astype(bf16)


def weight_grads(plan, lefts, mine, theirs, total=None, into=None, tile=256):
    tokens, width = lefts[0].shape
    kinds, _, columns = theirs.shape
    block = pl.BlockSpec((kinds, tokens, columns), lambda i: (0, 0, 0))
    made = len(plan) * columns
    place = 0 if into is None else into.shape[1] // made - 1
    total = total or (made if into is None else into.shape[1])
    operands = (*lefts, mine, theirs)
    call = pl.pallas_call(
        functools.partial(weight_grad_kernel, plan, len(lefts) // 2),
        out_shape=shape((width, total), bf16),
        grid=(width // tile,),
        in_specs=[pl.BlockSpec((tokens, tile), lambda i: (0, i))] * len(lefts)
        + [block] * 2
        + ([] if into is None else [pl.BlockSpec(memory_space=pl.ANY)]),
        out_specs=pl.BlockSpec((tile, made), lambda i: (i, place)),
        input_output_aliases={} if into is None else {len(operands): 0},
        compiler_params=pltpu.CompilerParams(vmem_limit_bytes=56 * MIB),
        cost_estimate=pl.CostEstimate(flops=1000, bytes_accessed=1000, transcendentals=0),
    )
    return call(*operands) if into is None else call(*operands, into)


def proj_grad_kernel(at_ref, n_ref, other_ref, mine, theirs, w_ref, out_ref, gain_ref):
    width = mine.shape[2]
    total = 0.0
    for k in range(3):
        columns = slice(k * width, (k + 1) * width)
        grad = mm(n_ref[...], mine[k], c_toks) + mm(other_ref[...], theirs[k], c_toks)
        out_ref[:, columns] = grad.astype(bf16)
        at = (k + 2) % 3 * width
        total = total + grad * w_ref[:, at : at + width].astype(f32)
    gain_ref[...] = ones_dot(jnp.ones((8, width), bf16), total, c_cols)


def proj_grads(at, normed, other, mine, theirs, w, tile=1024):
    tokens, width = normed.shape
    kinds, _, columns = theirs.shape
    left = pl.BlockSpec((tokens, tile), lambda i, _: (0, i))
    right = whole((kinds, tokens, columns))
    rows = pl.BlockSpec((tile, kinds * columns), lambda i, _: (i, 0))
    return kernel_call(
        proj_grad_kernel,
        (shape((width, kinds * columns), bf16), shape((8, width), f32)),
        (width // tile,),
        [
            left,
            left,
            right,
            right,
            pl.BlockSpec((None, tile, kinds * columns), lambda i, p: (half_of(p, 0), i, 0)),
        ],
        [rows, pl.BlockSpec((8, tile), lambda i, _: (0, i))],
        prefetch=1,
    )(at, normed, other, mine, theirs, w)


def norm_back(v, gain, grad):
    scale = lax.rsqrt(jnp.mean(v * v, axis=-1, keepdims=True) + norm_eps)
    scaled = grad * gain
    inner = jnp.mean(scaled * v, axis=-1, keepdims=True)
    grad_v = scale * scaled - v * (scale * scale * scale * inner)
    return grad_v, jnp.sum(grad * v * scale, axis=0, keepdims=True)


def norm2_kernel(parts_ref, resid_ref, dy_ref, g_ref, grad_ref, sent_ref, gain_ref):
    grad = sum(parts_ref[r].astype(f32) for r in range(RING))
    grad_v, gain = norm_back(resid_ref[...], g_ref[...], grad)
    total = dy_ref[...].astype(f32) + grad_v
    grad_ref[...] = total
    for r in range(RING):
        sent_ref[r] = total.astype(bf16)
    gain_ref[...] = gain


def norm2_back(parts, resid, dy, gain):
    dims = resid.shape
    return kernel_call(
        norm2_kernel,
        (shape(dims, f32), shape((RING,) + dims, bf16), shape(gain.shape, f32)),
        (1,),
        [whole(parts.shape), whole(dims), whole(dims), whole(gain.shape)],
        [whole(dims), whole((RING,) + dims), whole(gain.shape)],
    )(parts, resid, dy, gain)


def norm1_kernel(*refs):
    x_ref, g_ref, grad_resid_ref, out_ref = refs[RING:]
    grad = sum(refs[r][...].astype(f32) for r in range(RING))
    grad_v, _ = norm_back(x_ref[...].astype(f32), g_ref[...], grad)
    out_ref[...] = (grad_resid_ref[...] + grad_v).astype(bf16)


def norm1_back(parts, x, gain, grad_resid):
    dims = x.shape
    return kernel_call(
        norm1_kernel,
        shape(dims, bf16),
        (1,),
        [whole(dims)] * RING + [whole(dims), whole(gain.shape), whole(dims)],
        whole(dims),
    )(*parts, x, gain, grad_resid)


def unmix_kernel(
    place_ref,
    grad_ref,
    w_ref,
    mixed_ref,
    v_ref,
    qd_ref,
    decay_ref,
    taps_ref,
    gm_ref,
    gv_ref,
    gain_ref,
    added_ref,
    packed_ref,
):
    grad_gated = mm(grad_ref[...], w_ref[...], c_rows)
    gain = taps_ref[3 * KER + 1, :][None]
    mixed, v = mixed_ref[...], v_ref[...]
    scale = lax.rsqrt(jnp.mean(mixed * mixed, axis=-1, keepdims=True) + norm_eps)
    scaled = mixed * scale
    sig = sigmoid(v)
    silu = v * sig
    gain_ref[...] = jnp.broadcast_to(jnp.sum(grad_gated * scaled * silu, axis=0, keepdims=True), gain_ref.shape)
    gv_ref[...] = grad_gated * scaled * gain * (sig * (1.0 + v * (1.0 - sig)))
    grad_scaled = grad_gated * gain * silu
    inner = jnp.mean(grad_scaled * mixed, axis=-1, keepdims=True)
    gm_ref[...] = scale * grad_scaled - mixed * (scale * scale * scale * inner)
    state = jnp.zeros((HEAD_DIM, HEAD_DIM), f32)
    group = jnp.ones((HEAD_DIM, HEAD_DIM), f32)
    for n in range(mixed_ref.shape[0] // SPAN - 1, -1, -1):
        rows = pl.ds(n * SPAN, SPAN)
        added = mm(qd_ref[rows, :], gm_ref[rows, :], c_toks)
        added_ref[0, n] = added
        state = added + decay_ref[0, n] * state
        group = group * decay_ref[0, n]
    parts = packed_ref.shape[0]
    keys = HEAD_DIM // parts
    packed_ref[:, 0, :keys, :] = state.reshape(parts, keys, HEAD_DIM)
    packed_ref[:, 0, keys:, :] = group.reshape(parts, keys, HEAD_DIM)


def unmix(place, grad, w, mixed, v, qd, decay, taps, groups):
    tokens, channels = mixed.shape
    heads, blocks = decay.shape[:2]
    keys = HEAD_DIM // groups
    width = w.shape[1]
    first = w.shape[2] // HEAD_DIM - RING * 2

    def per_h(dims):
        return pl.BlockSpec(dims, lambda h, _: (0, h))

    def per_u(n):
        return pl.BlockSpec((1, n, HEAD_DIM, HEAD_DIM), lambda h, _: (h, 0, 0, 0))

    return kernel_call(
        unmix_kernel,
        (
            shape((tokens, channels), f32),
            shape((tokens, channels), f32),
            shape((8, channels), f32),
            shape(decay.shape, f32),
            shape((groups, heads, 2 * keys, HEAD_DIM), f32),
        ),
        (heads,),
        [
            whole(grad.shape),
            pl.BlockSpec(
                (None, width, HEAD_DIM), lambda h, p: (half_of(p, h // 2), 0, first + p[0] * 2 + h % 2)
            ),
            per_h((tokens, HEAD_DIM)),
            per_h((tokens, HEAD_DIM)),
            per_h((tokens, HEAD_DIM)),
            per_u(blocks),
            per_h((taps.shape[0], HEAD_DIM)),
        ],
        [
            per_h((tokens, HEAD_DIM)),
            per_h((tokens, HEAD_DIM)),
            per_h((8, HEAD_DIM)),
            per_u(blocks),
            pl.BlockSpec((groups, 1, 2 * keys, HEAD_DIM), lambda h, _: (0, h, 0, 0)),
        ],
        prefetch=1,
    )(place, grad, w, mixed, v, qd, decay, taps)


def recur_kernel(
    pq,
    pf,
    pi,
    hq,
    hf,
    hi,
    qc_ref,
    fc_ref,
    v_ref,
    cum_ref,
    qd_ref,
    kd_ref,
    gm_ref,
    gv_ref,
    enter_ref,
    added_ref,
    decay_ref,
    state_ref,
    taps_ref,
    grad_a_ref,
    grad_b_ref,
    tail_ref,
    halo_ref,
    small_ref,
    ext,
    gq,
    gf,
    gi,
):
    tokens = qc_ref.shape[0]
    gap = taps_ref[3 * KER, :][None]
    lower = triangle(True)
    triu = jnp.where(triangle(False), 1.0, 0.0).astype(bf16)
    ones = jnp.ones((8, HEAD_DIM), bf16)
    grad_gap = jnp.zeros((1, HEAD_DIM), f32)
    leaving = state_ref[...].reshape(HEAD_DIM, HEAD_DIM)
    for n in range(tokens // SPAN - 1, -1, -1):
        rows = pl.ds(n * SPAN, SPAN)
        qc, fc, v, cum = qc_ref[rows, :], fc_ref[rows, :], v_ref[rows, :], cum_ref[rows, :]
        q_dec, k_dec, grad = qd_ref[rows, :], kd_ref[rows, :], gm_ref[rows, :]
        entering = enter_ref[0, n]
        last = cum[SPAN - 1 :, :]
        sig = sigmoid(-fc)
        key = gap * sig
        rest = jnp.exp(last - cum)
        k_last = key * rest
        grad_scores = jnp.where(lower, mm(grad, v, c_cols), 0.0)
        scores = jnp.where(lower, mm(q_dec, k_dec, c_cols), 0.0)
        grad_qd = mm(grad_scores, k_dec, c_rows) + mm(grad, entering, c_cols)
        grad_kd = mm(grad_scores, q_dec, c_toks)
        grad_v = mm(scores, grad, c_toks) + mm(k_last, leaving, c_rows)
        grad_kl = mm(v, leaving, c_cols)
        through_last = grad_kl * k_last
        grad_decay = ones_dot(ones, entering * leaving, c_cols)[:1, :]
        grad_cum = grad_qd * q_dec.astype(f32) - grad_kd * k_dec.astype(f32) - through_last
        grad_last = jnp.sum(through_last, axis=0, keepdims=True) + grad_decay * jnp.exp(last)
        grad_log = ones_dot(triu, grad_cum, c_rows) + grad_last
        grad_key = grad_kd * jnp.exp(-cum) + grad_kl * rest - grad_log / (1.0 - key)
        grad_gap = grad_gap + jnp.sum(grad_key * sig, axis=0, keepdims=True)
        sig_q = sigmoid(qc)
        at = pl.ds(EDGE + n * SPAN, SPAN)
        gq[at, :] = grad_qd * jnp.exp(cum) * (sig_q * (1.0 + qc * (1.0 - sig_q)))
        gf[at, :] = -grad_key * key * (1.0 - sig)
        gi[at, :] = grad_v + gv_ref[rows, :]
        leaving = added_ref[0, n] + decay_ref[0, n] * leaving
    small_ref[...] = jnp.zeros(small_ref.shape, f32)
    small_ref[3 * KER : 3 * KER + 1, :] = grad_gap
    edge = jnp.zeros((EDGE, HEAD_DIM), f32)
    for branch, (g, proj, halo) in enumerate(((gq, pq, hq), (gf, pf, hf), (gi, pi, hi))):
        g[0:EDGE, :] = edge
        g[EDGE + tokens :, :] = edge
        total = 0.0
        before = 0.0
        ext[0:EDGE, :] = halo[...].astype(f32)
        ext[EDGE:, :] = proj[...].astype(f32)
        own = g[EDGE : EDGE + tokens, :]
        for j in range(KER):
            tap = taps_ref[branch * KER + j, :][None]
            shift = KER - 1 - j
            total = total + tap * g[EDGE + shift : EDGE + shift + tokens, :]
            before = before + tap * g[shift : shift + EDGE, :]
            row = branch * KER + j
            small_ref[row : row + 1, :] = jnp.sum(
                own * ext[EDGE - shift : EDGE - shift + tokens, :], axis=0, keepdims=True
            )
        first_half = pl.program_id(0) < pl.num_programs(0) // 2

        @pl.when(first_half)
        def _():
            grad_a_ref[branch] = total.astype(bf16)

        @pl.when(jnp.logical_not(first_half))
        def _():
            grad_b_ref[branch] = total.astype(bf16)

        tail_ref[branch] = total[tokens - EDGE :, :]
        halo_ref[branch] = before.astype(bf16)


def recur_back(pq, hq, proj, halo, qc, fc, v, cum, qd, kd, gm, gv, entering, added, decay, state, taps):
    tokens, channels = qc.shape
    heads, blocks = decay.shape[:2]
    rows = taps.shape[0]

    def kinds(n):
        return pl.BlockSpec((3, n, HEAD_DIM), lambda h: (0, 0, h))

    return kernel_call(
        recur_kernel,
        (
            shape((3, tokens, channels // 2), bf16),
            shape((3, tokens, channels // 2), bf16),
            shape((3, EDGE, channels), f32),
            shape((3, EDGE, channels), bf16),
            shape((rows, channels), f32),
        ),
        (heads,),
        [pl.BlockSpec((tokens, HEAD_DIM), place_of(k)) for k in range(3)]
        + [pl.BlockSpec((EDGE, HEAD_DIM), place_of(k)) for k in range(3)]
        + [per_head(tokens)] * 8
        + [per_unit(blocks)] * 3
        + [
            pl.BlockSpec((state.shape[0], 1) + state.shape[2:], lambda h: (0, h, 0, 0)),
            pl.BlockSpec((rows, HEAD_DIM), lambda h: (0, h)),
        ],
        [
            pl.BlockSpec((3, tokens, HEAD_DIM), lambda h: (0, 0, jnp.minimum(h, heads // 2 - 1))),
            pl.BlockSpec((3, tokens, HEAD_DIM), lambda h: (0, 0, jnp.maximum(h - heads // 2, 0))),
            kinds(EDGE),
            kinds(EDGE),     pl.BlockSpec((rows, HEAD_DIM), lambda h: (0, h)),
        ],
        scratch=[pltpu.VMEM((tokens + EDGE, HEAD_DIM), f32)]
        + [pltpu.VMEM((tokens + 2 * EDGE, HEAD_DIM), f32)] * 3,
    )(pq, proj, proj, hq, halo, halo, qc, fc, v, cum, qd, kd, gm, gv, entering, added, decay, state, taps)


def project_back_kernel(place_ref, da_ref, db_ref, wa_ref, wb_ref, *refs):
    held = refs[-1]
    part = da_ref.shape[2]
    total = 0.0
    for k in range(3):
        at = (k + 2) % 3 * part
        total = total + mm(da_ref[k], wa_ref[:, at : at + part], c_cols)
        total = total + mm(db_ref[k], wb_ref[:, at : at + part], c_cols)
    held[...] = total.astype(bf16)
    for r in range(RING):
        refs[r][...] = held[slot(place_ref, r), :]


def project_back(at, da, db, w, tile=1024):
    _, tokens, _ = da.shape
    _, width, columns = w.shape
    weights = [pl.BlockSpec((None, tile, columns), lambda i, p, k=k: (half_of(p, k), i, 0)) for k in range(2)]
    return kernel_call(
        project_back_kernel,
        tuple(shape((SPAN, width), bf16) for _ in range(RING)),
        (width // tile,),
        [whole(da.shape)] * 2 + weights,
        [pl.BlockSpec((SPAN, tile), lambda i, _: (0, i))] * RING,
        scratch=[pltpu.VMEM((tokens, tile), bf16)],
        prefetch=1,
    )(at, da, db, w, w)


def to_sequence(block, head):
    mine = lax.dynamic_index_in_dim(block, head, 0, False)
    other = swap(lax.dynamic_index_in_dim(block, 1 - head, 0, False))
    first = head == 0
    return jnp.concatenate((jnp.where(first, mine, other), jnp.where(first, other, mine)), axis=1)


def from_sequence(block, head):
    half = block.shape[1] // 2
    mine = lax.dynamic_slice_in_dim(block, head * half, half, 1)
    other = swap(lax.dynamic_slice_in_dim(block, (1 - head) * half, half, 1))
    first = head == 0
    return jnp.stack((jnp.where(first, mine, other), jnp.where(first, other, mine)))


def for_y(w):
    rows, columns = w.shape
    return w.reshape(rows, RING, columns // RING).transpose(1, 0, 2)


def after(value, *earlier):
    return lax.optimization_barrier((value, *earlier))[0]


def body(
    layer_input,
    w_q,
    w_f,
    w_i,
    conv_weight,
    forget_gap,
    gain_out,
    w_o,
    gain_attn,
    gain_ffn,
    w_gate,
    w_up,
    w_down,
    out_grad,
):
    head = lax.axis_index("head")
    place = lax.axis_index("y")
    at = jnp.stack((place, head)).astype(jnp.int32)
    groups = lax.axis_size(PLANE)
    length = layer_input.shape[1]
    width = 2 * layer_input.shape[2]
    part = w_q.shape[1] // RING
    ff_part = w_gate.shape[1] // RING
    ff_wide = pl.cdiv(ff_part, 256) * 256
    rows = w_q.shape[0]
    tokens = RING * length
    heads = 2 * part // HEAD_DIM

    def ff_columns(w):
        return jnp.pad(for_y(w), ((0, 0), (0, 0), (0, ff_wide - ff_part)))

    def gather(packed):
        held = exchange(packed, "y").reshape(RING * rows, -1)
        return held, lambda v: lax.all_gather(v, ("head",) + PLANE, axis=0, tiled=True).reshape(2, width, -1)

    x_own = to_sequence(layer_input, head)
    dy_own = to_sequence(out_grad, head)
    held, gathered = gather(jnp.concatenate([for_y(w) for w in (w_f, w_i, w_q)], axis=2))
    w_attn = gathered(held)
    packed = jnp.concatenate(
        [ff_columns(w) for w in (w_gate, w_up, w_down.T)]
        + [jnp.broadcast_to(w_o.T[None], (RING, rows, RING * part))],
        axis=2,
    )
    held, gathered = gather(after(packed, held))
    w_rest = gathered(held)
    x_blocks = ring_gather(x_own)
    route = [(i, i + 1) for i in range(groups - 1)]
    last = lax.dynamic_index_in_dim(
        jnp.stack([v[length - EDGE :] for v in x_blocks]), (RING - 1 - place) % RING, 0, False
    )
    x_before = lax.ppermute(last, PLANE, route)
    dy_blocks = ring_gather(after(dy_own, *x_blocks))

    def own_channels(v):
        return lax.dynamic_slice_in_dim(v, place * part, part, v.ndim - 1)

    small_own = jnp.concatenate(
        (
            own_channels(conv_weight).reshape(3 * KER, part),
            own_channels(forget_gap)[None],
            own_channels(gain_out)[None],
            jnp.zeros((2, part), bf16),
        )
    )
    taps = jnp.concatenate((small_own, swap(small_own)), axis=1).astype(f32)
    gains_own = jnp.stack((gain_attn, gain_ffn))
    gains_other = swap(gains_own)
    gains = jnp.where(
        head == 0,
        jnp.concatenate((gains_own, gains_other), axis=1),
        jnp.concatenate((gains_other, gains_own), axis=1),
    ).astype(f32)
    g_attn, g_ffn = gains[:1], gains[1:]

    normed, edge, proj, halo = project(at, x_blocks, x_before, g_attn, w_attn, 2 * part)
    fc, v, cum, kd, added, decay, packed = local_part(proj, halo, taps, heads, groups)
    proj_q, halo_q = project_more(at, after(normed, packed), edge, w_attn, part)
    dy_all = assemble(at, [after(v, packed) for v in dy_blocks])
    qc, qd, intra = query_part(proj_q, halo_q, taps, v, cum, kd)
    held = after(exchange(packed, PLANE), proj_q)
    state = after(exchange(scan_states(held, False), PLANE), intra, dy_all)
    gated, mixed, entering = mix(qd, v, intra, added, decay, state, taps)
    normed2, resid = attend(at, exchange(gated, "y"), w_rest, x_blocks, g_ffn)

    units_a, units_b = hidden_units(at, normed2, dy_all, w_rest, ff_wide)

    def split(v):
        return v.reshape(RING, length, width)

    grad_normed2 = units_back(at, ((1, 0), (2, 1)), units_a, units_b, w_rest)
    ff_grad = weight_grads(
        ((0, 1), (0, 2), (1, 0)),
        (after(normed2, grad_normed2), swap(normed2), dy_all, swap(dy_all)),
        units_a,
        swap(units_b),
        total=3 * ff_wide + part,
    )
    ffn = units_back(at, ((0, 2),), units_a, after(units_b, grad_normed2), w_rest, True)
    grad_normed2 = after(exchange(split(grad_normed2), "y"), ff_grad, ffn[0])

    grad_resid, sent, grad_g_ffn = norm2_back(grad_normed2, resid, dy_own, g_ffn)
    grad_attn = exchange(sent, "y").reshape(tokens, width)
    gm, gv, grad_gain, added_back, packed = unmix(
        at, grad_attn, w_rest, mixed, v, qd, decay, taps, groups
    )
    held = exchange(packed, PLANE)
    late_grad = after(grad_attn, held)
    rest_grad = weight_grads(
        ((0, 0),),
        (late_grad, swap(grad_attn)),
        gated[:1, :, :part],
        swap(gated[:1, :, part:]),
        into=ff_grad,
    )
    rest_sum = lax.psum_scatter(rest_grad, PLANE, scatter_dimension=0, tiled=True)
    state = after(exchange(scan_states(held, True), PLANE), rest_grad)
    ffn = [after(v, grad_attn) for v in ffn]
    output = (resid + sum(v.astype(f32) for v in ring_scatter(ffn))).astype(bf16)
    output = from_sequence(output, head)
    grads_a, grads_b, tail, before, small = recur_back(
        proj_q, halo_q, proj, halo, qc, fc, v, cum, qd, kd, gm, gv, entering, added_back, decay, state, taps
    )
    route = [(i + 1, i) for i in range(groups - 1)]
    sent_back = lax.ppermute(before, PLANE, route)
    tail = (tail + sent_back.astype(f32)).astype(bf16)
    grads_a = lax.dynamic_update_slice(grads_a, tail[:, :, :part], (0, tokens - EDGE, 0))
    grads_b = lax.dynamic_update_slice(grads_b, tail[:, :, part:], (0, tokens - EDGE, 0))
    proj_grad, grad_g_attn = proj_grads(at, normed, swap(normed), grads_a, swap(grads_b), w_attn)
    grad_g_attn = grad_g_attn[:1] / g_attn
    proj_sum = exchange(proj_grad.reshape(-1, rows, 3 * part), SEQ)
    parts = project_back(at, after(grads_a, proj_grad, output), grads_b, w_attn)
    input_grad = norm1_back(ring_scatter(parts), x_own, g_attn, grad_resid)

    per_channel = jnp.concatenate((small[: 3 * KER + 1], grad_gain[:1]))
    per_feature = jnp.concatenate((grad_g_attn, grad_g_ffn))
    half = width // 2
    own = lax.dynamic_slice_in_dim(per_feature, head * half, half, 1)
    other = lax.dynamic_slice_in_dim(per_feature, (1 - head) * half, half, 1)

    def spread(v, rest):
        return jnp.concatenate(
            (lax.dynamic_update_slice(jnp.zeros((v.shape[0], half), f32), v, (0, place * part)), rest)
        )

    small_grad = spread(per_channel[:, :part], own) + swap(spread(per_channel[:, part:], other))
    small_grad = axis_sum(axis_sum(after(small_grad, parts[0]), "y"), "z")
    input_grad = from_sequence(input_grad, head)

    rest_sum = ring_exchange(rest_sum.reshape(RING, rows, -1), place).astype(f32)
    proj_sum = after(proj_sum, input_grad, small_grad, rest_sum)
    small_grad = axis_sum(after(small_grad, proj_sum), "x")
    proj_sum = jnp.sum(proj_sum.reshape(groups, RING, rows, 3 * part).astype(f32), axis=0)

    def columns(v):
        return v.transpose(1, 0, 2).reshape(rows, -1)

    def turned(v):
        return v.transpose(0, 2, 1).reshape(-1, rows)

    grad_w = [columns(proj_sum[:, :, j * part : (j + 1) * part]) for j in range(3)]
    grad_w_gate, grad_w_up = columns(rest_sum[:, :, :ff_part]), columns(rest_sum[:, :, ff_wide : ff_wide + ff_part])
    grad_w_down = turned(rest_sum[:, :, 2 * ff_wide : 2 * ff_wide + ff_part])
    grad_w_o = turned(rest_sum[:, :, 3 * ff_wide :])
    return (
        output,
        input_grad,
        grad_w[0],
        grad_w[1],
        grad_w[2],
        small_grad[: 3 * KER].reshape(3, KER, half),
        small_grad[3 * KER],
        small_grad[3 * KER + 1],
        grad_w_o,
        small_grad[3 * KER + 2],
        small_grad[3 * KER + 3],
        grad_w_gate,
        grad_w_up,
        grad_w_down,
    )


def solution(mesh):
    fine = Mesh(mesh.devices.reshape(4, 4, RING, 2), ("x", "z", "y", "head"))
    tokens = P(None, SEQ, "head")
    rows = P(SEQ, "head")
    columns = P("head", SEQ)
    channels = P("head")
    taps = P(None, None, "head")
    return jax.shard_map(
        body,
        mesh=fine,
        in_specs=(
            tokens,
            rows,
            rows,
            rows,
            taps,
            channels,
            channels,
            columns,
            channels,
            channels,
            rows,
            rows,
            columns,
            tokens,
        ),
        out_specs=(
            tokens,
            tokens,
            rows,
            rows,
            rows,
            taps,
            channels,
            channels,
            columns,
            channels,
            channels,
            rows,
            rows,
            columns,
        ),
        check_vma=False,
    )
```

```python
import functools

import jax
import jax.numpy as jnp
from jax import lax
from jax.experimental import pallas as pl
from jax.experimental.pallas import tpu as pltpu
from jax.sharding import Mesh
from jax.sharding import PartitionSpec as P

HEAD_DIM = 128
KER = 4
SPAN = 128
RING = 4
EDGE = 16
PLANE = ("x", "z")
SEQ = ("x", "z", "y")

norm_eps = 1e-06
f32 = jnp.float32
bf16 = jnp.bfloat16
MIB = 1 << 20

c_rows = (((1,), (0,)), ((), ()))
c_cols = (((1,), (1,)), ((), ()))
c_toks = (((0,), (0,)), ((), ()))


def swap(block):
    return lax.ppermute(block, "head", [(0, 1), (1, 0)])


def exchange(block, axis):
    return lax.all_to_all(block, axis, 0, 0, tiled=True)


def from_ring(block, r):
    return lax.ppermute(block, "y", [((i + r) % RING, i) for i in range(RING)])


def ring_gather(block):
    return [block] + [from_ring(block, r) for r in range(1, RING)]


def ring_scatter(parts):
    return [parts[0]] + [from_ring(parts[r], RING - r) for r in range(1, RING)]


def ring_exchange(parts, place):
    sent = [lax.dynamic_index_in_dim(parts, (place - r) % RING, 0, False) for r in range(RING)]
    got = [sent[0]] + [from_ring(sent[r], r) for r in range(1, RING)]
    return lax.dynamic_slice_in_dim(jnp.stack(got + got), (RING - place) % RING, RING, 0)


def axis_sum(v, axis):
    count = lax.axis_size(axis)
    others = [lax.ppermute(v, axis, [((i + r) % count, i) for i in range(count)]) for r in range(1, count)]
    return sum(others, v)


def half_of(at_ref, k):
    return lax.rem(at_ref[1] + k, 2)


def slot(place_ref, r):
    return pl.ds(pl.multiple_of(lax.rem(place_ref[0] + r, RING) * SPAN, SPAN), SPAN)


def mm(a, b, contract):
    return lax.dot_general(a.astype(bf16), b.astype(bf16), contract, preferred_element_type=f32)


def ones_dot(ones, v, contract):
    high = v.astype(bf16)
    rest = v - high.astype(f32)
    middle = rest.astype(bf16)
    low = (rest - middle.astype(f32)).astype(bf16)
    return sum(
        lax.dot_general(ones, part, contract, preferred_element_type=f32) for part in (low, middle, high)
    )


def kernel_call(body, out_shape, grid, in_specs, out_specs, scratch=(), vmem=56, prefetch=0, weight=1):
    return pl.pallas_call(
        body,
        out_shape=out_shape,
        grid_spec=pltpu.PrefetchScalarGridSpec(
            num_scalar_prefetch=prefetch,
            grid=grid,
            in_specs=in_specs,
            out_specs=out_specs,
            scratch_shapes=list(scratch),
        ),
        compiler_params=pltpu.CompilerParams(vmem_limit_bytes=vmem * MIB),
        cost_estimate=pl.CostEstimate(flops=1000 * weight, bytes_accessed=1000 * weight, transcendentals=0),
    )


def shape(dims, dtype):
    return jax.ShapeDtypeStruct(tuple(dims), dtype)


def whole(dims):
    return pl.BlockSpec(tuple(dims), lambda *_: (0,) * len(dims))


def sigmoid(v):
    return 1.0 / (1.0 + jnp.exp(-v))


def triangle(lower):
    row = lax.broadcasted_iota(jnp.int32, (SPAN, SPAN), 0)
    col = lax.broadcasted_iota(jnp.int32, (SPAN, SPAN), 1)
    return row >= col if lower else row <= col


def project_kernel(place_ref, *refs):
    x_refs = refs[:RING]
    before_ref, g_ref, w_ref, normed_ref, edge_ref, proj_ref, halo_ref = refs[RING:]

    def norm(v):
        return (v * lax.rsqrt(jnp.mean(v * v, axis=-1, keepdims=True) + norm_eps) * g_ref[...]).astype(bf16)

    @pl.when(pl.program_id(0) == 0)
    def _():
        for r in range(RING):
            normed_ref[slot(place_ref, r), :] = norm(x_refs[r][...].astype(f32))
        edge_ref[...] = norm(before_ref[...].astype(f32))

    proj_ref[...] = mm(normed_ref[...], w_ref[...], c_rows).astype(bf16)
    halo_ref[...] = mm(edge_ref[...], w_ref[...], c_rows).astype(bf16)


def project(at, blocks, before, gain, w, columns):
    length, width = blocks[0].shape
    tokens = RING * length
    return kernel_call(
        project_kernel,
        (
            shape((tokens, width), bf16),
            shape((EDGE, width), bf16),
            shape((tokens, 2 * columns), bf16),
            shape((EDGE, 2 * columns), bf16),
        ),
        (2,),
        [whole(blocks[0].shape)] * RING
        + [
            whole(before.shape),
            whole(gain.shape),
            pl.BlockSpec((None, width, columns), lambda i, p: (half_of(p, i), 0, 0)),
        ],
        [
            whole((tokens, width)),
            whole((EDGE, width)),
            pl.BlockSpec((tokens, columns), lambda i, _: (0, i)),
            pl.BlockSpec((EDGE, columns), lambda i, _: (0, i)),
        ],
        prefetch=1,
    )(at, *blocks, before, gain, w)


def project_more_kernel(at_ref, n_ref, edge_ref, wa_ref, wb_ref, proj_ref, halo_ref):
    columns = wa_ref.shape[1]
    for k, w_ref in enumerate((wa_ref, wb_ref)):
        at = slice(k * columns, (k + 1) * columns)
        proj_ref[:, at] = mm(n_ref[...], w_ref[...], c_rows).astype(bf16)
        halo_ref[:, at] = mm(edge_ref[...], w_ref[...], c_rows).astype(bf16)


def project_more(at, normed, edge, w, columns):
    tokens, width = normed.shape
    last = w.shape[2] // columns - 1
    dims = ((tokens, 2 * columns), (EDGE, 2 * columns))
    return kernel_call(
        project_more_kernel,
        tuple(shape(d, bf16) for d in dims),
        (1,),
        [whole(normed.shape), whole(edge.shape)]
        + [pl.BlockSpec((None, width, columns), lambda i, p, k=k: (half_of(p, k), 0, last)) for k in range(2)],
        [whole(d) for d in dims],
        prefetch=1,
    )(at, normed, edge, w, w)


def assemble_kernel(place_ref, *refs):
    for r in range(RING):
        refs[-1][slot(place_ref, r), :] = refs[r][...]


def assemble(place, blocks):
    length, width = blocks[0].shape
    return kernel_call(
        assemble_kernel,
        shape((RING * length, width), blocks[0].dtype),
        (1,),
        [whole(blocks[0].shape)] * RING,
        whole((RING * length, width)),
        vmem=16,
        prefetch=1,
    )(place, *blocks)


def place_of(branch):
    if branch == 0:
        return lambda h: (0, h)
    return lambda h: (0, (h // 2) * 4 + (branch - 1) * 2 + h % 2)


def conv_of(ext, proj_ref, halo_ref, taps_ref, branch, tokens):
    ext[0:EDGE, :] = halo_ref[...].astype(f32)
    ext[EDGE:, :] = proj_ref[...].astype(f32)
    first = EDGE - (KER - 1)
    total = taps_ref[branch * KER, :][None] * ext[first : first + tokens, :]
    for j in range(1, KER):
        tap = taps_ref[branch * KER + j, :][None]
        total = total + tap * ext[first + j : first + j + tokens, :]
    return total


def spread_out(row):
    return jnp.transpose(jnp.broadcast_to(row, (HEAD_DIM, HEAD_DIM)))


def local_kernel(pf, pi, hf, hi, taps_ref, fc_ref, v_ref, cum_ref, kd_ref, added_ref, decay_ref, packed_ref, ext):
    tokens = pf.shape[0]
    fc_ref[...] = conv_of(ext, pf, hf, taps_ref, 1, tokens)
    v_ref[...] = conv_of(ext, pi, hi, taps_ref, 2, tokens)
    gap = taps_ref[3 * KER, :][None]
    tril = jnp.where(triangle(True), 1.0, 0.0).astype(bf16)
    state = jnp.zeros((HEAD_DIM, HEAD_DIM), f32)
    group = jnp.ones((HEAD_DIM, HEAD_DIM), f32)
    for n in range(tokens // SPAN):
        rows = pl.ds(n * SPAN, SPAN)
        f, v = fc_ref[rows, :], v_ref[rows, :]
        key = gap * sigmoid(-f)
        cum = ones_dot(tril, jnp.log1p(-key), c_rows)
        last = cum[SPAN - 1 :, :]
        decay = spread_out(jnp.exp(last))
        added = mm(key * jnp.exp(last - cum), v, c_toks)
        cum_ref[rows, :] = cum
        kd_ref[rows, :] = (key * jnp.exp(-cum)).astype(bf16)
        added_ref[0, n] = added
        decay_ref[0, n] = decay
        state = added + decay * state
        group = group * decay
    parts = packed_ref.shape[0]
    keys = HEAD_DIM // parts
    packed_ref[:, 0, :keys, :] = state.reshape(parts, keys, HEAD_DIM)
    packed_ref[:, 0, keys:, :] = group.reshape(parts, keys, HEAD_DIM)


def per_head(tokens):
    return pl.BlockSpec((tokens, HEAD_DIM), lambda h: (0, h))


def per_unit(blocks):
    return pl.BlockSpec((1, blocks, HEAD_DIM, HEAD_DIM), lambda h: (h, 0, 0, 0))


def local_part(proj, halo, taps, heads, groups):
    tokens = proj.shape[0]
    blocks = tokens // SPAN
    flat = (tokens, heads * HEAD_DIM)
    units = (heads, blocks, HEAD_DIM, HEAD_DIM)
    keys = HEAD_DIM // groups
    packed = (groups, heads, 2 * keys, HEAD_DIM)
    return kernel_call(
        local_kernel,
        (
            *(shape(flat, f32) for _ in range(3)),
            shape(flat, bf16),
            shape(units, f32),
            shape(units, f32),
            shape(packed, f32),
        ),
        (heads,),
        [pl.BlockSpec((tokens, HEAD_DIM), place_of(k)) for k in (1, 2)]
        + [pl.BlockSpec((EDGE, HEAD_DIM), place_of(k)) for k in (1, 2)]
        + [pl.BlockSpec((taps.shape[0], HEAD_DIM), lambda h: (0, h))],
        [per_head(tokens)] * 4
        + [per_unit(blocks)] * 2
        + [pl.BlockSpec((groups, 1, 2 * keys, HEAD_DIM), lambda h: (0, h, 0, 0))],
        scratch=[pltpu.VMEM((tokens + EDGE, HEAD_DIM), f32)],
    )(proj, proj, halo, halo, taps)


def query_kernel(pq, hq, taps_ref, v_ref, cum_ref, kd_ref, qc_ref, qd_ref, intra_ref, ext):
    tokens = pq.shape[0]
    qc_ref[...] = conv_of(ext, pq, hq, taps_ref, 0, tokens)
    lower = triangle(True)
    for n in range(tokens // SPAN):
        rows = pl.ds(n * SPAN, SPAN)
        q = qc_ref[rows, :]
        q_dec = (q * sigmoid(q) * jnp.exp(cum_ref[rows, :])).astype(bf16)
        scores = jnp.where(lower, mm(q_dec, kd_ref[rows, :], c_cols), 0.0)
        intra_ref[rows, :] = mm(scores, v_ref[rows, :], c_rows)
        qd_ref[rows, :] = q_dec


def query_part(proj, halo, taps, v, cum, kd):
    tokens, channels = v.shape
    return kernel_call(
        query_kernel,
        (shape(v.shape, f32), shape(v.shape, bf16), shape(v.shape, f32)),
        (channels // HEAD_DIM,),
        [per_head(tokens), per_head(EDGE), per_head(taps.shape[0])] + [per_head(tokens)] * 3,
        [per_head(tokens)] * 3,
        scratch=[pltpu.VMEM((tokens + EDGE, HEAD_DIM), f32)],
    )(proj, halo, taps, v, cum, kd)


def scan_kernel(reverse, state_ref, decay_ref, out_ref):
    groups, _, keys, _ = out_ref.shape
    state = jnp.zeros(out_ref.shape[1:], f32)
    for g in range(groups - 1, -1, -1) if reverse else range(groups):
        out_ref[g] = state
        state = state_ref[g, :, :keys, :] + decay_ref[g, :, keys:, :] * state


def scan_states(states, decays, reverse):
    groups, heads, double, width = decays.shape
    dims = (groups, heads, double // 2, width)
    return kernel_call(
        functools.partial(scan_kernel, reverse),
        shape(dims, f32),
        (1,),
        [whole(states.shape), whole(decays.shape)],
        whole(dims),
        vmem=16,
        weight=10**6 if reverse else 1,
    )(states, decays)


def mix_kernel(
    qd_ref,
    v_ref,
    intra_ref,
    added_ref,
    decay_ref,
    state_ref,
    taps_ref,
    gated_ref,
    late_ref,
    mixed_ref,
    enter_ref,
):
    state = state_ref[...].reshape(HEAD_DIM, HEAD_DIM)
    gain = taps_ref[3 * KER + 1, :][None]
    for n in range(qd_ref.shape[0] // SPAN):
        rows = pl.ds(n * SPAN, SPAN)
        enter_ref[0, n] = state
        mixed = intra_ref[rows, :] + mm(qd_ref[rows, :], state, c_rows)
        state = added_ref[0, n] + decay_ref[0, n] * state
        mixed_ref[rows, :] = mixed
        v = v_ref[rows, :]
        scale = lax.rsqrt(jnp.mean(mixed * mixed, axis=-1, keepdims=True) + norm_eps)
        gated = (mixed * scale * gain * (v * sigmoid(v))).astype(bf16)
        late_ref[0, rows, :] = gated
        for r in range(RING):
            gated_ref[r, rows, :] = gated


def mix(qd, v, intra, added, decay, state, taps):
    tokens, channels = qd.shape
    heads, blocks = added.shape[:2]
    return kernel_call(
        mix_kernel,
        (
            shape((RING, tokens, channels), bf16),
            shape((1, tokens, channels // 2), bf16),
            shape((tokens, channels), f32),
            shape(added.shape, f32),
        ),
        (heads,),
        [per_head(tokens)] * 3
        + [per_unit(blocks)] * 2
        + [
            pl.BlockSpec((state.shape[0], 1) + state.shape[2:], lambda h: (0, h, 0, 0)),
            pl.BlockSpec((taps.shape[0], HEAD_DIM), lambda h: (0, h)),
        ],
        [
            pl.BlockSpec((RING, tokens, HEAD_DIM), lambda h: (0, 0, h)),
            pl.BlockSpec((1, tokens, HEAD_DIM), lambda h: (0, 0, jnp.maximum(h - heads // 2, 0))),
            per_head(tokens),
            per_unit(blocks),
        ],
    )(qd, v, intra, added, decay, state, taps)


def feed_kernel(at_ref, gathered, w, *refs):
    x_refs, refs = refs[:RING], refs[RING:]
    dy_ref, g_ref, normed_out, resid_ref, ua_out, ub_out, back_out, *refs = refs
    lefts, x, dy, weights, held, normed, ua, ub, back, left_sem, x_sem, o_sem, w_sem, out_sem = refs
    part = gathered.shape[2] // 2
    inner = RING * part
    width = w.shape[1]
    columns = ua.shape[2]
    tile, wide = 512, 256
    tiles, half = width // tile, columns // wide
    mine = half_of(at_ref, 0)

    def half_at(k):
        return mine if k == 0 else 1 - mine

    def o_copy(k, t):
        rows = pl.ds(t * tile, tile)
        return pltpu.make_async_copy(
            w.at[half_at(k), rows, pl.ds(0, inner)], weights.at[k, rows, pl.ds(0, inner)], o_sem.at[k, t]
        )

    def w_copy(k, j, t):
        at = pl.ds(inner + j * columns + t * wide, wide)
        return pltpu.make_async_copy(w.at[half_at(k), :, at], weights.at[k, :, at], w_sem.at[k, j, t])

    def w_tile(n):
        return [w_copy(n // half, j, n % half) for j in range(3)]

    left_copies = [
        pltpu.make_async_copy(
            gathered.at[s, :, pl.ds(k * part, part)], lefts.at[k, :, pl.ds(s * part, part)], left_sem.at[k, s]
        )
        for k in range(2)
        for s in range(RING)
    ]
    x_copies = [
        pltpu.make_async_copy(x_refs[r], x.at[slot(at_ref, r), :], x_sem.at[r]) for r in range(RING)
    ]
    dy_copy = pltpu.make_async_copy(dy_ref, dy, x_sem.at[RING])
    for c in left_copies + [o_copy(0, 0), o_copy(1, 0)] + x_copies + [o_copy(0, 1), o_copy(1, 1)]:
        c.start()
    for c in left_copies:
        c.wait()

    square = jnp.zeros((x.shape[0], 1), f32)
    for t in range(tiles):
        for k in range(2):
            o_copy(k, t).wait()
        if t == 0:
            for c in x_copies:
                c.wait()
        if t + 2 < tiles:
            o_copy(0, t + 2).start()
            o_copy(1, t + 2).start()
        elif t + 2 == tiles:
            dy_copy.start()
            for c in w_tile(0):
                c.start()
        else:
            for c in w_tile(1):
                c.start()
        rows, cols = slice(t * tile, (t + 1) * tile), slice(t * tile, (t + 1) * tile)
        total = x[:, cols].astype(f32)
        for k in range(2):
            total = total + mm(lefts[k], weights[k, rows, :inner], c_cols)
        held[:, cols] = total
        square = square + jnp.sum(total * total, axis=-1, keepdims=True)
    scale = lax.rsqrt(square / width + norm_eps)
    for t in range(tiles):
        cols = slice(t * tile, (t + 1) * tile)
        normed[:, cols] = (held[:, cols] * scale * g_ref[:, cols]).astype(bf16)
        resid_ref[:, cols] = held[slot(at_ref, 0), cols]
    normed_copy = pltpu.make_async_copy(normed, normed_out, out_sem.at[0])
    normed_copy.start()
    dy_copy.wait()

    for n in range(2 * half):
        k, t = n // half, n % half
        for c in w_tile(n):
            c.wait()
        if n + 2 < 2 * half:
            for c in w_tile(n + 2):
                c.start()
        at = [slice(inner + j * columns + t * wide, inner + j * columns + (t + 1) * wide) for j in range(3)]
        gate = mm(normed[...], weights[k, :, at[0]], c_rows)
        up = mm(normed[...], weights[k, :, at[1]], c_rows)
        grad = mm(dy[...], weights[k, :, at[2]], c_rows)
        sig = sigmoid(gate)
        silu = gate * sig
        cols = slice(t * wide, (t + 1) * wide)
        u = (ua, ub)[k]
        u[0, :, cols] = (silu * up).astype(bf16)
        u[1, :, cols] = (grad * up * (sig * (1.0 + gate * (1.0 - sig)))).astype(bf16)
        u[2, :, cols] = (grad * silu).astype(bf16)
    unit_copies = [
        pltpu.make_async_copy(ua, ua_out, out_sem.at[1]),
        pltpu.make_async_copy(ub, ub_out, out_sem.at[2]),
    ]
    for c in unit_copies:
        c.start()

    back_copies = []
    for t in range(tiles):
        rows, cols = slice(t * tile, (t + 1) * tile), slice(t * tile, (t + 1) * tile)
        total = 0.0
        for k, u in enumerate((ua, ub)):
            for j in range(2):
                at = slice(inner + j * columns, inner + (j + 1) * columns)
                total = total + mm(u[1 + j], weights[k, rows, at], c_cols)
        back[t] = total.astype(bf16)
        c = pltpu.make_async_copy(back.at[t], back_out.at[:, pl.ds(t * tile, tile)], out_sem.at[3 + t])
        c.start()
        back_copies.append(c)
    for c in [normed_copy] + unit_copies + back_copies:
        c.wait()


def feed(at, gathered, w, x, gain, dy, columns):
    _, tokens, channels = gathered.shape
    length, width = x[0].shape
    inner = RING * channels // 2
    tiles, half = width // 512, columns // 256
    away = pl.BlockSpec(memory_space=pl.ANY)
    return kernel_call(
        feed_kernel,
        (
            shape((tokens, width), bf16),
            shape((length, width), f32),
            shape((3, tokens, columns), bf16),
            shape((3, tokens, columns), bf16),
            shape((tokens, width), bf16),
        ),
        (1,),
        [away] * (2 + RING + 1) + [whole(gain.shape)],
        [away, whole((length, width)), away, away, away],
        scratch=[
            pltpu.VMEM((2, tokens, inner), bf16),
            pltpu.VMEM((tokens, width), bf16),
            pltpu.VMEM((tokens, width), bf16),
            pltpu.VMEM((2, width, inner + 3 * columns), bf16),
            pltpu.VMEM((tokens, width), f32),
            pltpu.VMEM((tokens, width), bf16),
            pltpu.VMEM((3, tokens, columns), bf16),
            pltpu.VMEM((3, tokens, columns), bf16),
            pltpu.VMEM((tiles, tokens, 512), bf16),
            pltpu.SemaphoreType.DMA((2, RING)),
            pltpu.SemaphoreType.DMA((RING + 1,)),
            pltpu.SemaphoreType.DMA((2, tiles)),
            pltpu.SemaphoreType.DMA((2, 3, half)),
            pltpu.SemaphoreType.DMA((3 + tiles,)),
        ],
        vmem=60,
        prefetch=1,
    )(at, gathered, w, *x, dy, gain)


def down_kernel(at_ref, ua_ref, ub_ref, *refs):
    held = refs[-1]
    wide = refs[0].shape[1]
    count = ua_ref.shape[2] // wide
    total = 0.0
    for k, u_ref in enumerate((ua_ref, ub_ref)):
        for t in range(count):
            total = total + mm(u_ref[0, :, t * wide : (t + 1) * wide], refs[k * count + t][...], c_cols)
    held[...] = total.astype(bf16)
    for r in range(RING):
        refs[2 * count + r][...] = held[slot(at_ref, r), :]


def down(at, ua, ub, w, tile=512, wide=256):
    _, tokens, columns = ua.shape
    width = w.shape[1]
    count = columns // wide
    first = w.shape[2] // wide - count
    return kernel_call(
        down_kernel,
        tuple(shape((SPAN, width), bf16) for _ in range(RING)),
        (width // tile,),
        [pl.BlockSpec((1, tokens, columns), lambda i, _: (0, 0, 0))] * 2
        + [
            pl.BlockSpec((None, tile, wide), lambda i, p, k=k, t=t: (half_of(p, k), i, first + t))
            for k in range(2)
            for t in range(count)
        ],
        [pl.BlockSpec((SPAN, tile), lambda i, _: (0, i))] * RING,
        scratch=[pltpu.VMEM((tokens, tile), bf16)],
        prefetch=1,
    )(at, ua, ub, *[w] * (2 * count))


def beside(ref, kinds):
    return jnp.concatenate([ref[k] for k in kinds], axis=1) if len(kinds) > 1 else ref[kinds[0]]


def weight_grad_kernel(plan, *refs):
    mine, theirs = refs[2 * len(plan) : 2 * len(plan) + 2]
    out_ref = refs[-1]
    at = 0
    for n, kinds in enumerate(plan):
        grad = mm(refs[2 * n][...], beside(mine, kinds), c_toks)
        grad = grad + mm(refs[2 * n + 1][...], beside(theirs, kinds), c_toks)
        out_ref[:, at : at + grad.shape[1]] = grad.astype(bf16)
        at += grad.shape[1]


def weight_grads(plan, lefts, mine, theirs, into=None, tile=256):
    tokens, width = lefts[0].shape
    _, _, columns = theirs.shape
    made = sum(len(kinds) for kinds in plan) * columns
    operands = (*lefts, mine, theirs) + (() if into is None else (into,))
    return pl.pallas_call(
        functools.partial(weight_grad_kernel, plan),
        out_shape=shape((width, made) if into is None else into.shape, bf16),
        grid=(width // tile,),
        in_specs=[pl.BlockSpec((tokens, tile), lambda i: (0, i))] * len(lefts)
        + [whole(theirs.shape)] * 2
        + ([] if into is None else [pl.BlockSpec(memory_space=pl.ANY)]),
        out_specs=pl.BlockSpec((tile, made), lambda i: (i, 0)),
        input_output_aliases={} if into is None else {len(operands) - 1: 0},
        compiler_params=pltpu.CompilerParams(vmem_limit_bytes=56 * MIB),
        cost_estimate=pl.CostEstimate(flops=1000, bytes_accessed=1000, transcendentals=0),
    )(*operands)


def late_grad_kernel(ga_ref, gb_ref, na_ref, nb_ref, oa_ref, ob_ref, qa_ref, qb_ref, out_ref):
    @pl.when(pl.program_id(0) == 0)
    def _():
        out_ref[...] = (mm(ga_ref[...], oa_ref[0], c_toks) + mm(gb_ref[...], ob_ref[0], c_toks)).astype(bf16)

    @pl.when(pl.program_id(0) == 1)
    def _():
        out_ref[...] = (mm(na_ref[...], qa_ref[...], c_toks) + mm(nb_ref[...], qb_ref[...], c_toks)).astype(bf16)


def late_grads(grad_attn, normed, gated, grads, tile=1024):
    tokens, width = normed[0].shape
    columns = grads[0].shape[1]
    steps = width // tile
    return kernel_call(
        late_grad_kernel,
        shape((width, 4 * columns), bf16),
        (2, steps),
        [pl.BlockSpec((tokens, tile), lambda j, i: (0, i * (1 - j) + (steps - 1) * j))] * 2
        + [pl.BlockSpec((tokens, tile), lambda j, i: (0, i * j))] * 2
        + [pl.BlockSpec((1, tokens, columns), lambda j, i: (0, 0, 0))] * 2
        + [pl.BlockSpec((tokens, columns), lambda j, i: (0, 0))] * 2,
        pl.BlockSpec((tile, columns), lambda j, i: (i, 2 + j)),
    )(*grad_attn, *normed, *gated, *grads)


def norm_back(v, gain, grad):
    scale = lax.rsqrt(jnp.mean(v * v, axis=-1, keepdims=True) + norm_eps)
    scaled = grad * gain
    inner = jnp.mean(scaled * v, axis=-1, keepdims=True)
    grad_v = scale * scaled - v * (scale * scale * scale * inner)
    return grad_v, jnp.sum(grad * v * scale, axis=0, keepdims=True)


def norm2_kernel(parts_ref, resid_ref, dy_ref, g_ref, grad_ref, sent_ref, gain_ref):
    grad = sum(parts_ref[r].astype(f32) for r in range(RING))
    grad_v, gain = norm_back(resid_ref[...], g_ref[...], grad)
    total = dy_ref[...].astype(f32) + grad_v
    grad_ref[...] = total
    for r in range(RING):
        sent_ref[r] = total.astype(bf16)
    gain_ref[...] = gain


def norm2_back(parts, resid, dy, gain):
    dims = resid.shape
    return kernel_call(
        norm2_kernel,
        (shape(dims, f32), shape((RING,) + dims, bf16), shape(gain.shape, f32)),
        (1,),
        [whole(parts.shape), whole(dims), whole(dims), whole(gain.shape)],
        [whole(dims), whole((RING,) + dims), whole(gain.shape)],
    )(parts, resid, dy, gain)


def put_parted(at_ref, total, keep_ref, send_ref):
    half = total.shape[1] // 2
    for h in range(2):

        @pl.when(at_ref[1] == h)
        def _():
            keep_ref[...] = total[:, h * half : (h + 1) * half]
            send_ref[...] = total[:, (1 - h) * half : (2 - h) * half]


def norm1_kernel(at_ref, *refs):
    x_ref, g_ref, grad_resid_ref, keep_ref, send_ref = refs[RING:]
    grad = sum(refs[r][...].astype(f32) for r in range(RING))
    grad_v, _ = norm_back(x_ref[...].astype(f32), g_ref[...], grad)
    put_parted(at_ref, (grad_resid_ref[...] + grad_v).astype(bf16), keep_ref, send_ref)


def norm1_back(at, parts, x, gain, grad_resid):
    dims = x.shape
    half = (dims[0], dims[1] // 2)
    return kernel_call(
        norm1_kernel,
        (shape(half, bf16), shape(half, bf16)),
        (1,),
        [whole(dims)] * RING + [whole(dims), whole(gain.shape), whole(dims)],
        [whole(half)] * 2,
        prefetch=1,
    )(at, *parts, x, gain, grad_resid)


def output_kernel(at_ref, *refs):
    resid_ref, keep_ref, send_ref = refs[RING:]
    total = resid_ref[...]
    for r in range(RING):
        total = total + refs[r][...].astype(f32)
    put_parted(at_ref, total.astype(bf16), keep_ref, send_ref)


def summed_output(at, parts, resid):
    dims = resid.shape
    half = (dims[0], dims[1] // 2)
    return kernel_call(
        output_kernel,
        (shape(half, bf16), shape(half, bf16)),
        (1,),
        [whole(dims)] * (RING + 1),
        [whole(half)] * 2,
        prefetch=1,
    )(at, *parts, resid)


def unmix_kernel(
    place_ref,
    grad_ref,
    w_ref,
    mixed_ref,
    v_ref,
    qd_ref,
    decay_ref,
    taps_ref,
    gm_ref,
    gv_ref,
    gain_ref,
    added_ref,
    packed_ref,
):
    grad_gated = mm(grad_ref[...], w_ref[...], c_rows)
    gain = taps_ref[3 * KER + 1, :][None]
    mixed, v = mixed_ref[...], v_ref[...]
    scale = lax.rsqrt(jnp.mean(mixed * mixed, axis=-1, keepdims=True) + norm_eps)
    scaled = mixed * scale
    sig = sigmoid(v)
    silu = v * sig
    gain_ref[...] = jnp.broadcast_to(jnp.sum(grad_gated * scaled * silu, axis=0, keepdims=True), gain_ref.shape)
    gv_ref[...] = grad_gated * scaled * gain * (sig * (1.0 + v * (1.0 - sig)))
    grad_scaled = grad_gated * gain * silu
    inner = jnp.mean(grad_scaled * mixed, axis=-1, keepdims=True)
    gm_ref[...] = scale * grad_scaled - mixed * (scale * scale * scale * inner)
    state = jnp.zeros((HEAD_DIM, HEAD_DIM), f32)
    for n in range(mixed_ref.shape[0] // SPAN - 1, -1, -1):
        rows = pl.ds(n * SPAN, SPAN)
        added = mm(qd_ref[rows, :], gm_ref[rows, :], c_toks)
        added_ref[0, n] = added
        state = added + decay_ref[0, n] * state
    packed_ref[...] = state.reshape(packed_ref.shape)


def unmix(place, grad, w, mixed, v, qd, decay, taps, groups):
    tokens, channels = mixed.shape
    heads, blocks = decay.shape[:2]
    keys = HEAD_DIM // groups
    width = w.shape[1]

    def per_h(dims):
        return pl.BlockSpec(dims, lambda h, _: (0, h))

    def per_u(n):
        return pl.BlockSpec((1, n, HEAD_DIM, HEAD_DIM), lambda h, _: (h, 0, 0, 0))

    return kernel_call(
        unmix_kernel,
        (
            shape((tokens, channels), f32),
            shape((tokens, channels), f32),
            shape((8, channels), f32),
            shape(decay.shape, f32),
            shape((groups, heads, keys, HEAD_DIM), f32),
        ),
        (heads,),
        [
            whole(grad.shape),
            pl.BlockSpec(
                (None, width, HEAD_DIM), lambda h, p: (half_of(p, h // 2), 0, p[0] * 2 + h % 2)
            ),
            per_h((tokens, HEAD_DIM)),
            per_h((tokens, HEAD_DIM)),
            per_h((tokens, HEAD_DIM)),
            per_u(blocks),
            per_h((taps.shape[0], HEAD_DIM)),
        ],
        [
            per_h((tokens, HEAD_DIM)),
            per_h((tokens, HEAD_DIM)),
            per_h((8, HEAD_DIM)),
            per_u(blocks),
            pl.BlockSpec((groups, 1, keys, HEAD_DIM), lambda h, _: (0, h, 0, 0)),
        ],
        prefetch=1,
    )(place, grad, w, mixed, v, qd, decay, taps)


def conv_back(grad, ext, proj_ref, halo_ref, taps_ref, branch, tokens):
    edge = jnp.zeros((EDGE, HEAD_DIM), f32)
    grad[0:EDGE, :] = edge
    grad[EDGE + tokens :, :] = edge
    ext[0:EDGE, :] = halo_ref[...].astype(f32)
    ext[EDGE:, :] = proj_ref[...].astype(f32)
    own = grad[EDGE : EDGE + tokens, :]
    total, before, taps = 0.0, 0.0, []
    for j in range(KER):
        tap = taps_ref[branch * KER + j, :][None]
        shift = KER - 1 - j
        total = total + tap * grad[EDGE + shift : EDGE + shift + tokens, :]
        before = before + tap * grad[shift : shift + EDGE, :]
        taps.append(jnp.sum(own * ext[EDGE - shift : EDGE - shift + tokens, :], axis=0, keepdims=True))
    return total, before, taps


def put_halves(total, a_ref, b_ref):
    first_half = pl.program_id(0) < pl.num_programs(0) // 2

    @pl.when(first_half)
    def _():
        a_ref[...] = total.astype(bf16)

    @pl.when(jnp.logical_not(first_half))
    def _():
        b_ref[...] = total.astype(bf16)


def halves(dims, heads):
    lead = (0,) * (len(dims) - 1)
    return [
        pl.BlockSpec((*dims, HEAD_DIM), lambda h: (*lead, 0, jnp.minimum(h, heads // 2 - 1))),
        pl.BlockSpec((*dims, HEAD_DIM), lambda h: (*lead, 0, jnp.maximum(h - heads // 2, 0))),
    ]


def within_kernel(
    pq,
    hq,
    qc_ref,
    cum_ref,
    taps_ref,
    v_ref,
    qd_ref,
    kd_ref,
    gm_ref,
    enter_ref,
    dq_ref,
    dk_ref,
    dv_ref,
    grad_a_ref,
    grad_b_ref,
    tail_ref,
    before_ref,
    small_ref,
    ext,
    gq,
):
    tokens = v_ref.shape[0]
    lower = triangle(True)
    for n in range(tokens // SPAN):
        rows = pl.ds(n * SPAN, SPAN)
        q_dec, k_dec = qd_ref[rows, :], kd_ref[rows, :]
        grad = gm_ref[rows, :].astype(bf16)
        grad_scores = jnp.where(lower, mm(grad, v_ref[rows, :], c_cols), 0.0).astype(bf16)
        scores = jnp.where(lower, mm(q_dec, k_dec, c_cols), 0.0)
        grad_qd = mm(grad_scores, k_dec, c_rows) + mm(grad, enter_ref[0, n], c_cols)
        dq_ref[rows, :] = grad_qd * q_dec.astype(f32)
        dk_ref[rows, :] = mm(grad_scores, q_dec, c_toks)
        dv_ref[rows, :] = mm(scores, grad, c_toks)
        qc = qc_ref[rows, :]
        sig = sigmoid(qc)
        gq[pl.ds(EDGE + n * SPAN, SPAN), :] = grad_qd * jnp.exp(cum_ref[rows, :]) * (sig * (1.0 + qc * (1.0 - sig)))
    total, before, taps = conv_back(gq, ext, pq, hq, taps_ref, 0, tokens)
    small_ref[...] = jnp.zeros(small_ref.shape, f32)
    for j, tap in enumerate(taps):
        small_ref[j : j + 1, :] = tap
    put_halves(total, grad_a_ref, grad_b_ref)
    tail_ref[...] = total[tokens - EDGE :, :]
    before_ref[...] = before.astype(bf16)


def within_back(pq, hq, qc, cum, taps, v, qd, kd, gm, entering):
    tokens, channels = v.shape
    heads = channels // HEAD_DIM
    return kernel_call(
        within_kernel,
        (
            *(shape(v.shape, f32) for _ in range(3)),
            shape((tokens, channels // 2), bf16),
            shape((tokens, channels // 2), bf16),
            shape((EDGE, channels), f32),
            shape((EDGE, channels), bf16),
            shape((8, channels), f32),
        ),
        (heads,),
        [per_head(tokens), per_head(EDGE), per_head(tokens), per_head(tokens), per_head(taps.shape[0])]
        + [per_head(tokens)] * 4
        + [per_unit(tokens // SPAN)],
        [per_head(tokens)] * 3 + halves((tokens,), heads) + [per_head(EDGE), per_head(EDGE), per_head(8)],
        scratch=[
            pltpu.VMEM((tokens + EDGE, HEAD_DIM), f32),
            pltpu.VMEM((tokens + 2 * EDGE, HEAD_DIM), f32),
        ],
    )(pq, hq, qc, cum, taps, v, qd, kd, gm, entering)


def recur_kernel(
    pf,
    pi,
    hf,
    hi,
    fc_ref,
    v_ref,
    cum_ref,
    kd_ref,
    gv_ref,
    dq_ref,
    dk_ref,
    dv_ref,
    enter_ref,
    added_ref,
    decay_ref,
    state_ref,
    taps_ref,
    grad_a_ref,
    grad_b_ref,
    tail_ref,
    before_ref,
    small_ref,
    ext,
    gf,
    gi,
):
    tokens = fc_ref.shape[0]
    gap = taps_ref[3 * KER, :][None]
    triu = jnp.where(triangle(False), 1.0, 0.0).astype(bf16)
    ones = jnp.ones((8, HEAD_DIM), bf16)
    grad_gap = jnp.zeros((1, HEAD_DIM), f32)
    leaving = state_ref[...].reshape(HEAD_DIM, HEAD_DIM)
    for n in range(tokens // SPAN - 1, -1, -1):
        rows = pl.ds(n * SPAN, SPAN)
        fc, v, cum = fc_ref[rows, :], v_ref[rows, :], cum_ref[rows, :]
        grad_kd = dk_ref[rows, :]
        last = cum[SPAN - 1 :, :]
        sig = sigmoid(-fc)
        key = gap * sig
        rest = jnp.exp(last - cum)
        k_last = key * rest
        grad_v = dv_ref[rows, :] + mm(k_last, leaving, c_rows)
        grad_kl = mm(v, leaving, c_cols)
        through_last = grad_kl * k_last
        grad_decay = ones_dot(ones, enter_ref[0, n] * leaving, c_cols)[:1, :]
        grad_cum = dq_ref[rows, :] - grad_kd * kd_ref[rows, :].astype(f32) - through_last
        grad_last = jnp.sum(through_last, axis=0, keepdims=True) + grad_decay * jnp.exp(last)
        grad_log = ones_dot(triu, grad_cum, c_rows) + grad_last
        grad_key = grad_kd * jnp.exp(-cum) + grad_kl * rest - grad_log / (1.0 - key)
        grad_gap = grad_gap + jnp.sum(grad_key * sig, axis=0, keepdims=True)
        at = pl.ds(EDGE + n * SPAN, SPAN)
        gf[at, :] = -grad_key * key * (1.0 - sig)
        gi[at, :] = grad_v + gv_ref[rows, :]
        leaving = added_ref[0, n] + decay_ref[0, n] * leaving
    small_ref[...] = jnp.zeros(small_ref.shape, f32)
    small_ref[2 * KER : 2 * KER + 1, :] = grad_gap
    totals = []
    for branch, (g, proj, halo) in enumerate(((gf, pf, hf), (gi, pi, hi))):
        total, before, taps = conv_back(g, ext, proj, halo, taps_ref, branch + 1, tokens)
        for j, tap in enumerate(taps):
            small_ref[branch * KER + j : branch * KER + j + 1, :] = tap
        totals.append(total)
        tail_ref[branch] = total[tokens - EDGE :, :]
        before_ref[branch] = before.astype(bf16)
    put_halves(jnp.stack(totals), grad_a_ref, grad_b_ref)


def recur_back(proj, halo, fc, v, cum, kd, gv, dq, dk, dv, entering, added, decay, state, taps):
    tokens, channels = fc.shape
    heads, blocks = decay.shape[:2]
    rows = taps.shape[0]

    def kinds(n):
        return pl.BlockSpec((2, n, HEAD_DIM), lambda h: (0, 0, h))

    return kernel_call(
        recur_kernel,
        (
            shape((2, tokens, channels // 2), bf16),
            shape((2, tokens, channels // 2), bf16),
            shape((2, EDGE, channels), f32),
            shape((2, EDGE, channels), bf16),
            shape((16, channels), f32),
        ),
        (heads,),
        [pl.BlockSpec((tokens, HEAD_DIM), place_of(k)) for k in (1, 2)]
        + [pl.BlockSpec((EDGE, HEAD_DIM), place_of(k)) for k in (1, 2)]
        + [per_head(tokens)] * 8
        + [per_unit(blocks)] * 3
        + [
            pl.BlockSpec((state.shape[0], 1) + state.shape[2:], lambda h: (0, h, 0, 0)),
            pl.BlockSpec((rows, HEAD_DIM), lambda h: (0, h)),
        ],
        halves((2, tokens), heads) + [kinds(EDGE), kinds(EDGE), per_head(16)],
        scratch=[pltpu.VMEM((tokens + EDGE, HEAD_DIM), f32)]
        + [pltpu.VMEM((tokens + 2 * EDGE, HEAD_DIM), f32)] * 2,
    )(proj, proj, halo, halo, fc, v, cum, kd, gv, dq, dk, dv, entering, added, decay, state, taps)


def project_back_kernel(at_ref, qa_ref, qb_ref, da_ref, db_ref, n_ref, wa_ref, wb_ref, *refs):
    gain_ref, held = refs[RING:]
    total = 0.0
    for q_ref, d_ref, w_ref in ((qa_ref, da_ref, wa_ref), (qb_ref, db_ref, wb_ref)):
        grads = jnp.concatenate((d_ref[0], d_ref[1], q_ref[...]), axis=1)
        total = total + mm(grads, w_ref[...], c_cols)
    held[...] = total.astype(bf16)
    for r in range(RING):
        refs[r][...] = held[slot(at_ref, r), :]
    gain = jnp.sum(total * n_ref[...].astype(f32), axis=0, keepdims=True)
    gain_ref[...] = jnp.broadcast_to(gain, gain_ref.shape)


def project_back(at, qa, qb, da, db, normed, w, tile=512):
    _, tokens, _ = da.shape
    _, width, columns = w.shape
    *parts, gain = kernel_call(
        project_back_kernel,
        (*(shape((SPAN, width), bf16) for _ in range(RING)), shape((8, width), f32)),
        (width // tile,),
        [whole(qa.shape)] * 2
        + [whole(da.shape)] * 2
        + [pl.BlockSpec((tokens, tile), lambda i, _: (0, i))]
        + [pl.BlockSpec((None, tile, columns), lambda i, p, k=k: (half_of(p, k), i, 0)) for k in range(2)],
        [pl.BlockSpec((SPAN, tile), lambda i, _: (0, i))] * RING + [pl.BlockSpec((8, tile), lambda i, _: (0, i))],
        scratch=[pltpu.VMEM((tokens, tile), bf16)],
        prefetch=1,
    )(at, qa, qb, da, db, normed, w, w)
    return parts, gain


def total_kernel(parts_ref, out_ref):
    total = parts_ref[0].astype(f32)
    for g in range(1, parts_ref.shape[0]):
        total = total + parts_ref[g].astype(f32)
    out_ref[...] = total.astype(bf16)


def plane_total(parts):
    dims = parts.shape[1:]
    return kernel_call(total_kernel, shape(dims, bf16), (1,), [whole(parts.shape)], whole(dims))(parts)


def spread_kernel(parts_ref, *out_refs):
    width = parts_ref.shape[2] // len(out_refs)
    for y in range(RING):
        for k, out_ref in enumerate(out_refs):
            part = parts_ref[y, :, k * width : (k + 1) * width]
            out_ref[:, y * width : (y + 1) * width] = part.astype(f32)


def spread_grads(parts, count):
    _, rows, columns = parts.shape
    dims = (rows, RING * columns // count)
    return kernel_call(
        spread_kernel,
        tuple(shape(dims, f32) for _ in range(count)),
        (1,),
        [whole(parts.shape)],
        [whole(dims)] * count,
        weight=10**6,
    )(parts)


def to_sequence(block, head):
    mine = lax.dynamic_index_in_dim(block, head, 0, False)
    other = swap(lax.dynamic_index_in_dim(block, 1 - head, 0, False))
    first = head == 0
    return jnp.concatenate((jnp.where(first, mine, other), jnp.where(first, other, mine)), axis=1)


def from_sequence(keep, send, head):
    other = swap(send)
    first = head == 0
    return jnp.stack((jnp.where(first, keep, other), jnp.where(first, other, keep)))


def for_y(w):
    rows, columns = w.shape
    return w.reshape(rows, RING, columns // RING).transpose(1, 0, 2)


def after(value, *earlier):
    return lax.optimization_barrier((value, *earlier))[0]


def body(
    layer_input,
    w_q,
    w_f,
    w_i,
    conv_weight,
    forget_gap,
    gain_out,
    w_o,
    gain_attn,
    gain_ffn,
    w_gate,
    w_up,
    w_down,
    out_grad,
):
    head = lax.axis_index("head")
    place = lax.axis_index("y")
    at = jnp.stack((place, head)).astype(jnp.int32)
    groups = lax.axis_size(PLANE)
    length = layer_input.shape[1]
    width = 2 * layer_input.shape[2]
    part = w_q.shape[1] // RING
    ff_part = w_gate.shape[1] // RING
    ff_wide = pl.cdiv(ff_part, 256) * 256
    rows = w_q.shape[0]
    tokens = RING * length
    heads = 2 * part // HEAD_DIM

    def ff_columns(w):
        return jnp.pad(for_y(w), ((0, 0), (0, 0), (0, ff_wide - ff_part)))

    def gather(packed):
        held = exchange(packed, "y").reshape(RING * rows, -1)
        return held, lambda v: lax.all_gather(v, ("head",) + PLANE, axis=0, tiled=True).reshape(2, width, -1)

    x_own = to_sequence(layer_input, head)
    dy_own = to_sequence(out_grad, head)
    held, gathered = gather(jnp.concatenate([for_y(w) for w in (w_f, w_i, w_q)], axis=2))
    w_attn = gathered(held)
    packed = jnp.concatenate(
        [jnp.broadcast_to(w_o.T[None], (RING, rows, RING * part))]
        + [ff_columns(w) for w in (w_gate, w_up, w_down.T)],
        axis=2,
    )
    held, gathered = gather(after(packed, held))
    w_rest = gathered(held)
    x_blocks = ring_gather(x_own)
    route = [(i, i + 1) for i in range(groups - 1)]
    last = lax.dynamic_index_in_dim(
        jnp.stack([v[length - EDGE :] for v in x_blocks]), (RING - 1 - place) % RING, 0, False
    )
    x_before = lax.ppermute(last, PLANE, route)
    dy_blocks = ring_gather(after(dy_own, *x_blocks))

    def own_channels(v):
        return lax.dynamic_slice_in_dim(v, place * part, part, v.ndim - 1)

    small_own = jnp.concatenate(
        (
            own_channels(conv_weight).reshape(3 * KER, part),
            own_channels(forget_gap)[None],
            own_channels(gain_out)[None],
            jnp.zeros((2, part), bf16),
        )
    )
    taps = jnp.concatenate((small_own, swap(small_own)), axis=1).astype(f32)
    gains_own = jnp.stack((gain_attn, gain_ffn))
    gains_other = swap(gains_own)
    gains = jnp.where(
        head == 0,
        jnp.concatenate((gains_own, gains_other), axis=1),
        jnp.concatenate((gains_other, gains_own), axis=1),
    ).astype(f32)
    g_attn, g_ffn = gains[:1], gains[1:]

    normed, edge, proj, halo = project(at, x_blocks, x_before, g_attn, w_attn, 2 * part)
    fc, v, cum, kd, added, decay, packed = local_part(proj, halo, taps, heads, groups)
    proj_q, halo_q = project_more(at, after(normed, packed), edge, w_attn, part)
    dy_all = assemble(at, [after(v, packed) for v in dy_blocks])
    qc, qd, intra = query_part(proj_q, halo_q, taps, v, cum, kd)
    held = after(exchange(packed, PLANE), proj_q)
    decays = held
    state = after(exchange(scan_states(held, held, False), PLANE), intra, dy_all)
    gated, gated_b, mixed, entering = mix(qd, v, intra, added, decay, state, taps)
    normed2, resid, units_a, units_b, grad_normed2 = feed(
        at, exchange(gated, "y"), w_rest, x_blocks, g_ffn, dy_all, ff_wide
    )

    def split(v):
        return v.reshape(RING, length, width)

    ff_grad = weight_grads(
        ((1, 2), (0,)),
        (normed2, swap(normed2), dy_all, swap(dy_all)),
        units_a,
        swap(units_b),
    )
    ffn = down(at, units_a, units_b, w_rest)
    grad_normed2 = after(exchange(split(grad_normed2), "y"), ff_grad, ffn[0])

    grad_resid, sent, grad_g_ffn = norm2_back(grad_normed2, resid, dy_own, g_ffn)
    ff_sum = lax.psum_scatter(after(ff_grad, sent), PLANE, scatter_dimension=0, tiled=True)
    grad_attn = exchange(sent, "y").reshape(tokens, width)
    gm, gv, grad_gain, added_back, packed = unmix(
        at, grad_attn, w_rest, mixed, v, qd, decay, taps, groups
    )
    back_route = [(i + 1, i) for i in range(groups - 1)]
    crossed = [(2 * i + 3 - h, 2 * i + h) for i in range(groups - 1) for h in range(2)]

    def patched(grads, own, sent):
        edge = (own.astype(f32) + sent.astype(f32)).astype(bf16)
        return lax.dynamic_update_slice(grads, edge, (0,) * (grads.ndim - 2) + (tokens - EDGE, 0))

    def completed(grads_a, grads_b, tail, before):
        sent = lax.ppermute(before, PLANE, back_route)
        theirs_sent = lax.ppermute(before[..., part:], PLANE + ("head",), crossed)
        sent, theirs_sent, theirs = lax.optimization_barrier((sent, theirs_sent, swap(grads_b)))
        return (
            patched(grads_a, tail[..., :part], sent[..., :part]),
            patched(grads_b, tail[..., part:], sent[..., part:]),
            patched(theirs, theirs[..., tokens - EDGE :, :], theirs_sent),
        )

    dq, dk, dv, *query_grads, small_q = within_back(proj_q, halo_q, qc, cum, taps, v, qd, kd, gm, entering)
    held = after(exchange(packed, PLANE), dq)
    gq_a, gq_b, gq_theirs = completed(*query_grads)
    scanned = scan_states(held, decays, True)
    late_grad = late_grads(
        (after(grad_attn, scanned), swap(grad_attn)),
        (normed, swap(normed)),
        (gated, swap(gated_b)),
        (gq_a, gq_theirs),
    )
    state = after(exchange(scanned, PLANE), late_grad)
    ffn = ring_scatter([after(v, grad_attn) for v in ffn])
    *more_grads, small_fi = recur_back(
        proj, halo, fc, v, cum, kd, gv, dq, dk, dv, entering, added_back, decay, state, taps
    )
    g_a, g_b, g_theirs = completed(*more_grads)
    output = summed_output(at, ffn, after(resid, small_fi))
    g_a = after(g_a, g_theirs, output[0])
    parts, grad_g_attn = project_back(at, gq_a, gq_b, g_a, g_b, normed, w_attn)
    grad_g_attn = grad_g_attn[:1] / g_attn
    attn_grad = weight_grads(
        ((0, 1),), (after(normed, parts[0]), swap(normed)), g_a, g_theirs, into=late_grad, tile=1024
    )
    attn_sum = exchange(attn_grad.reshape(groups, RING * rows, 4 * part), PLANE)

    def columns(v):
        return v.transpose(1, 0, 2).reshape(rows, -1)

    def turned(v):
        return v.transpose(0, 2, 1).reshape(-1, rows)

    ff_sum = ring_exchange(ff_sum.reshape(RING, rows, -1), place).astype(f32)
    grad_w_gate, grad_w_up = columns(ff_sum[:, :, :ff_part]), columns(ff_sum[:, :, ff_wide : ff_wide + ff_part])
    grad_w_down = turned(ff_sum[:, :, 2 * ff_wide : 2 * ff_wide + ff_part])
    output = from_sequence(*output, head)
    input_grad = norm1_back(at, ring_scatter(parts), x_own, g_attn, grad_resid)
    attn_sum = plane_total(after(attn_sum, grad_w_gate, grad_w_up, grad_w_down, *input_grad))
    input_grad = [after(v, attn_sum) for v in input_grad]
    small = jnp.concatenate((small_q[:KER], small_fi[: 2 * KER + 1]))

    per_channel = jnp.concatenate((small[: 3 * KER + 1], grad_gain[:1]))
    per_feature = jnp.concatenate((grad_g_attn, grad_g_ffn))
    half = width // 2
    own = lax.dynamic_slice_in_dim(per_feature, head * half, half, 1)
    other = lax.dynamic_slice_in_dim(per_feature, (1 - head) * half, half, 1)

    def spread(v, rest):
        return jnp.concatenate(
            (lax.dynamic_update_slice(jnp.zeros((v.shape[0], half), f32), v, (0, place * part)), rest)
        )

    small_grad = spread(per_channel[:, :part], own) + swap(spread(per_channel[:, part:], other))
    small_grad = axis_sum(after(axis_sum(after(small_grad, attn_grad), "y"), attn_sum), "z")

    input_grad = from_sequence(*input_grad, head)

    attn_sum = exchange(attn_sum.reshape(RING, rows, 4 * part), "y")
    small_grad = axis_sum(after(small_grad, attn_sum), "x")
    grad_w_f, grad_w_i, grad_w_o, grad_w_q = spread_grads(attn_sum, 4)
    grad_w_o = grad_w_o.T
    return (
        output,
        input_grad,
        grad_w_q,
        grad_w_f,
        grad_w_i,
        small_grad[: 3 * KER].reshape(3, KER, half),
        small_grad[3 * KER],
        small_grad[3 * KER + 1],
        grad_w_o,
        small_grad[3 * KER + 2],
        small_grad[3 * KER + 3],
        grad_w_gate,
        grad_w_up,
        grad_w_down,
    )


def solution(mesh):
    fine = Mesh(mesh.devices.reshape(4, 4, RING, 2), ("x", "z", "y", "head"))
    tokens = P(None, SEQ, "head")
    rows = P(SEQ, "head")
    columns = P("head", SEQ)
    channels = P("head")
    taps = P(None, None, "head")
    return jax.shard_map(
        body,
        mesh=fine,
        in_specs=(
            tokens,
            rows,
            rows,
            rows,
            taps,
            channels,
            channels,
            columns,
            channels,
            channels,
            rows,
            rows,
            columns,
            tokens,
        ),
        out_specs=(
            tokens,
            tokens,
            rows,
            rows,
            rows,
            taps,
            channels,
            channels,
            columns,
            channels,
            channels,
            rows,
            rows,
            columns,
        ),
        check_vma=False,
    )
```
